32 devices in a mesh: dp: 2 (over core), wide: 16 (over z, y, x).
Axes of the slice: x: 2, y: 2, z: 4, core: 2. Of those that a mesh axis runs over, the one named last changes fastest.
Arguments:
- layer_in: bfloat16 [256, 4096], P('wide', 'dp'), may hold values from -6 to 6
- route_ids: int32 [256, 8], P('wide'), may hold values from 0 to 15, all different within a row; in each aligned block of 16 rows (0 to 15, 16 to 31, ...) at most 16 rows name the same one
- route_scores: float32 [256, 8], P('wide'), may hold values from 0.05 to 1
- expert_gate: bfloat16 [16, 1536, 4096], P('wide', None, 'dp'), may hold values from -0.09375 to 0.09375
- expert_up: bfloat16 [16, 1536, 4096], P('wide', None, 'dp'), may hold values from -0.09375 to 0.09375
- expert_down: bfloat16 [16, 1536, 4096], P('wide', None, 'dp'), may hold values from -0.15625 to 0.15625
- student_gate: bfloat16 [12288, 4096], P('wide', 'dp'), may hold values from -0.09375 to 0.09375
- student_up: bfloat16 [12288, 4096], P('wide', 'dp'), may hold values from -0.09375 to 0.09375
- student_down: bfloat16 [12288, 4096], P('wide', 'dp'), may hold values from -0.0546875 to 0.0546875
Outputs:
- teacher_out: bfloat16 [256, 4096], P('wide', 'dp')
- grad_gate: bfloat16 [12288, 4096], P('wide', 'dp')
- grad_up: bfloat16 [12288, 4096], P('wide', 'dp')
- grad_down: bfloat16 [12288, 4096], P('wide', 'dp')
The draws below stay inside these ranges and needn't reach their ends.
Inputs may be any that keep to these rules, and one draw needn't show every extreme that they name: `route_ids`: each row names 8 different experts. Within the 16 rows of one device no expert is named more than 16 times, a bound that some block reaches there.
All inputs are finite; a program needn't handle non-finite values.
Results may differ from the reference program's by a relative error of at most 0.0058.
Values may be sent and summed in bfloat16 or wider, within the bound.
No kernel may reach another device: no remote copies, remote signals or barrier semaphores. Data moves between devices by JAX's collectives and lax.ppermute only.
A program may use at most 128 MiB of HBM per device.

```python
import math
import jax
import jax.numpy as jnp
import numpy as np
from jax import lax

D = 4096
HID = 1536
TOP = 8
FF = 12288
TOK_W = 16
TOKENS = 256
EXPERTS = 16
CAP = 16
N_WIDE = 16


def levels(own_key, shape, cuts, least, top_value):
    def one(dim, shards_of):
        heights = jax.random.uniform(jax.random.fold_in(jax.random.fold_in(own_key, 6), dim), (shards_of,), jnp.float32, least / len(cuts), top_value / len(cuts))
        return jnp.repeat(jnp.exp(heights), shape[dim] // shards_of).reshape((-1,) + (1,) * (len(shape) - dim - 1))

    factor_of = one(*cuts[0])
    for cut in cuts[1:]:
        factor_of = factor_of * one(*cut)
    return factor_of


def assign_block(own_key, own, number, rows, count, top, bound, slope):
    order = jax.random.permutation(own_key, count)
    packed, ordinary = load_shares(count, rows * top, bound, slope, True), load_shares(count, rows * top, bound, slope, False)
    places = jnp.arange(count)

    def named(sizes, rotation):
        used = int((sizes > 0).sum())
        fixed = max(1, used // 4)
        moved = fixed + (places - fixed + rotation * (used - fixed)) % max(1, count - fixed)
        return jnp.zeros((count,), jnp.int32).at[order[jnp.where(places < fixed, places, moved)]].set(jnp.asarray(sizes, jnp.int32))

    sizes = jnp.where(number % 4 == 0, named(packed, number // 4), named(ordinary, number - number // 4 - 1))
    mixed = jax.random.permutation(jax.random.fold_in(own, 3), count)
    donor, sink = mixed[0:count // 2 * 2:2], mixed[1:count // 2 * 2:2]
    margin = jnp.minimum(sizes[donor] - 1, bound - sizes[sink]) // 2
    margin = jnp.where((donor == order[0]) | (sink == order[0]) | (sizes[sink] == 0), 0, jnp.maximum(margin, 0))
    moved = jax.random.randint(jax.random.fold_in(own, 4), (count // 2,), 0, 1 << 20) % (margin + 1)
    sizes = sizes.at[donor].add(-moved).at[sink].add(moved)
    labels = jnp.searchsorted(jnp.cumsum(sizes), jnp.arange(rows * top), side="right").astype(jnp.int32)
    table = labels.reshape(top, rows).T
    table = table[jax.random.permutation(jax.random.fold_in(own, 1), rows)]
    rotation = jax.random.randint(jax.random.fold_in(own, 2), (rows, 1), 0, top)
    return jnp.take_along_axis(table, (jnp.arange(top)[None, :] + rotation) % top, axis=1)


def load_shares(count, total, bound, skew, full):
    portions = [(1 << 20) // math.isqrt(grade ** skew) + 1 for grade in range(1, count + 1)]
    largest = bound if full else min(bound, max(-(-total // count), total * portions[0] // sum(portions)))
    least = 1 if total - largest >= count - 1 else 0
    given, surplus = [largest] + [least] * (count - 1), total - largest - least * (count - 1)
    while surplus > 0:
        candidates = [i for i in range(1, count) if given[i] < largest] or [i for i in range(1, count) if given[i] < bound]
        whole, budget = sum([portions[i] for i in candidates]), surplus
        for i in candidates:
            addition = min(bound - given[i], max(1, budget * portions[i] // whole), surplus)
            given[i] = given[i] + addition
            surplus = surplus - addition
    return np.array(given)


def scatter_about(stream_key, shape, spread, limit, shards=(), held_as=jnp.bfloat16):
    values = spread * jax.random.normal(stream_key, shape, jnp.float32)
    if shards:
        values = values * levels(stream_key, shape, shards, -0.22, 0.18)
    return jnp.clip(values, -limit, limit).astype(held_as)


def setup_inputs(seed: int = 0) -> dict:
    keys = jax.random.split(jax.random.key(seed), 10)
    layer_in = scatter_about(keys[0], (TOKENS, D), 1.0, 6.0, ((0, 16), (1, 2)))
    route_ids_keys = jax.random.split(jax.random.fold_in(keys[1], 1), TOKENS // TOK_W)
    route_ids_turns = jax.random.permutation(jax.random.fold_in(keys[1], 3), TOKENS // TOK_W)
    route_ids = jax.vmap(lambda own, number: assign_block(jax.random.fold_in(keys[1], 2), own, number, TOK_W, EXPERTS, TOP, CAP, 1))(route_ids_keys, route_ids_turns).reshape((TOKENS, TOP))
    route_scores = jnp.clip(jnp.exp(math.log(1.0) - 2.9957323 * jax.random.uniform(keys[2], (TOKENS, TOP), jnp.float32) ** levels(keys[2], (TOKENS, TOP), ((0, 16),), -0.2, 0.2)), 0.05, 1.0)
    expert_gate = scatter_about(keys[3], (EXPERTS, HID, D), D ** -0.5, 0.09375, ((0, 16), (2, 2)))
    expert_up = scatter_about(keys[4], (EXPERTS, HID, D), D ** -0.5, 0.09375, ((0, 16), (2, 2)))
    expert_down = scatter_about(keys[5], (EXPERTS, HID, D), HID ** -0.5, 0.15625, ((0, 16), (2, 2)))
    student_gate = scatter_about(keys[6], (FF, D), D ** -0.5, 0.09375, ((0, 16), (1, 2)))
    student_up = scatter_about(keys[7], (FF, D), D ** -0.5, 0.09375, ((0, 16), (1, 2)))
    student_down = scatter_about(keys[8], (FF, D), FF ** -0.5, 0.0546875, ((0, 16), (1, 2)))
    return {"layer_in": layer_in, "route_ids": route_ids, "route_scores": route_scores, "expert_gate": expert_gate, "expert_up": expert_up, "expert_down": expert_down, "student_gate": student_gate, "student_up": student_up, "student_down": student_down}


def silu_terms(values):
    sig_value = jax.nn.sigmoid(values)
    return (values * sig_value, sig_value)

def reference(layer_in, route_ids, route_scores, expert_gate, expert_up, expert_down, student_gate, student_up, student_down):
    route_weights = route_scores / lax.optimization_barrier(jnp.sum(route_scores, axis=1, keepdims=True))
    flat_ids = route_ids.reshape(-1).astype(jnp.int32)
    flat_weights = route_weights.reshape(-1)
    flat_tokens = (jnp.arange(TOKENS * TOP, dtype=jnp.int32) // TOP).astype(jnp.int32)
    most_rows = N_WIDE * CAP

    def one_expert(running, pieces):
        number, gate_mat, up_mat, down_mat = pieces
        is_taken = flat_ids == number
        slot_order = jnp.cumsum(is_taken.astype(jnp.int32)) - 1
        target = jnp.where(is_taken, slot_order, most_rows).astype(jnp.int32)
        token_of = jnp.zeros((most_rows,), jnp.int32).at[target].set(flat_tokens, mode='drop')
        weight_of = jnp.zeros((most_rows,), jnp.float32).at[target].set(flat_weights, mode='drop')
        picked_rows = layer_in[token_of]
        gate_pre = jnp.dot(picked_rows, gate_mat.T, preferred_element_type=jnp.float32)
        up_pre = jnp.dot(picked_rows, up_mat.T, preferred_element_type=jnp.float32)
        swished, _ = silu_terms(gate_pre)
        expert_hidden = (swished * up_pre).astype(jnp.bfloat16)
        expert_value = jnp.dot(expert_hidden, down_mat, preferred_element_type=jnp.float32).astype(jnp.bfloat16)
        running = running.at[token_of].add(weight_of[:, None] * expert_value.astype(jnp.float32))
        return (running, None)
    start_sum = jnp.zeros((TOKENS, D), jnp.float32)
    numbers = jnp.arange(EXPERTS, dtype=jnp.int32)
    summed, _ = lax.scan(one_expert, start_sum, (numbers, expert_gate, expert_up, expert_down))
    teacher_out = summed.astype(jnp.bfloat16)
    gate_pre = jnp.dot(layer_in, student_gate.T, preferred_element_type=jnp.float32)
    up_pre = jnp.dot(layer_in, student_up.T, preferred_element_type=jnp.float32)
    swished, sig_value = silu_terms(gate_pre)
    student_hidden = (swished * up_pre).astype(jnp.bfloat16)
    student_out = jnp.dot(student_hidden, student_down, preferred_element_type=jnp.float32)
    loss_scale = 1.0 / math.sqrt(TOKENS)
    delta_rows = (student_out - summed) * loss_scale
    grad_down = jnp.dot(student_hidden.astype(jnp.float32).T, delta_rows, precision=lax.Precision.HIGHEST, preferred_element_type=jnp.float32).astype(jnp.bfloat16)
    hidden_grad = jnp.dot(delta_rows, student_down.astype(jnp.float32).T, precision=lax.Precision.HIGHEST, preferred_element_type=jnp.float32)
    gate_grad_pre = (hidden_grad * up_pre * sig_value * (1.0 + gate_pre * (1.0 - sig_value))).astype(jnp.bfloat16)
    up_grad_pre = (hidden_grad * swished).astype(jnp.bfloat16)
    grad_gate = jnp.dot(gate_grad_pre.T, layer_in, preferred_element_type=jnp.float32).astype(jnp.bfloat16)
    grad_up = jnp.dot(up_grad_pre.T, layer_in, preferred_element_type=jnp.float32).astype(jnp.bfloat16)
    return (teacher_out, grad_gate, grad_up, grad_down)
```

```python
import functools
import math

import jax
import jax.numpy as jnp
from jax import lax
from jax.experimental import pallas as pl
from jax.experimental.pallas import tpu as pltpu
from jax.sharding import PartitionSpec as P

BF16 = jnp.bfloat16
F32 = jnp.float32
VMEM_LIMIT = 48 * 1024 * 1024
LANES = 128


def against(left_mat, right_mat):
    return lax.dot_general(left_mat, right_mat, (((1,), (1,)), ((), ())), preferred_element_type=F32)


def across(left_mat, right_mat):
    return lax.dot_general(left_mat, right_mat, (((0,), (0,)), ((), ())), preferred_element_type=F32)


def plain(left_mat, right_mat):
    return lax.dot_general(left_mat, right_mat, (((1,), (0,)), ((), ())), preferred_element_type=F32)


def block_of(size, most=256):
    fits = [b for b in range(LANES, most + 1, LANES) if size % b == 0]
    return fits[-1] if fits else size


def params():
    return pltpu.CompilerParams(vmem_limit_bytes=VMEM_LIMIT, dimension_semantics=("arbitrary",))


def cost(flops, nbytes):
    return pl.CostEstimate(flops=int(flops), bytes_accessed=int(nbytes), transcendentals=0)


class Ring:
    def __init__(self, size):
        inner = max(d for d in range(1, size + 1) if size % d == 0 and d * d <= size)
        self.size, self.inner, self.outer = size, inner, size // inner
        self.binary = size & (size - 1) == 0

    def add(self, index, near, far):
        if self.binary:
            return index ^ (near + self.inner * far)
        low, high = index % self.inner, index // self.inner
        return (low + near) % self.inner + self.inner * ((high + far) % self.outer)

    def fetch(self, value, near, far):
        return lax.ppermute(value, "wide", [(self.add(i, near, far), i) for i in range(self.size)])

    def send(self, value, near, far):
        return lax.ppermute(value, "wide", [(i, self.add(i, near, far)) for i in range(self.size)])

    def gather(self, value):
        column = [value] + [self.fetch(value, 0, k) for k in range(1, self.outer)]
        column = jnp.concatenate(column, axis=0)
        pieces = [column] + [self.fetch(column, k, 0) for k in range(1, self.inner)]
        return jnp.concatenate(pieces, axis=0)

    def reduce(self, pieces):
        arrived = [pieces[0]] + [self.send(pieces[k], k, 0) for k in range(1, self.inner)]
        column = sum(a.astype(F32) for a in arrived).astype(BF16)
        column = column.reshape(self.outer, column.shape[0] // self.outer, column.shape[1])
        arrived = [column[0]] + [self.send(column[k], 0, k) for k in range(1, self.outer)]
        return sum(a.astype(F32) for a in arrived)


def from_pair(value):
    size = lax.axis_size("dp")
    return [lax.ppermute(value, "dp", [(i, (i + s) % size) for i in range(size)]) for s in range(1, size)]


def payload_kernel(owners, layer_ref, ids_ref, scores_ref, out_ref):
    rows, columns = layer_ref.shape
    out_ref[:, :columns] = layer_ref[...]
    scores = scores_ref[...]
    weights = scores / jnp.sum(scores, axis=0, keepdims=True)
    ids = ids_ref[...]
    shape = (out_ref.shape[1] - columns, rows)
    place = lax.broadcasted_iota(jnp.int32, shape, 0)
    expert = jnp.where(place >= owners, place - owners, place)
    table = jnp.zeros(shape, F32)
    for k in range(ids.shape[0]):
        table = table + jnp.where(ids[k : k + 1, :] == expert, weights[k : k + 1, :], 0.0)
    high = table.astype(BF16).astype(F32)
    table = jnp.where(place < owners, high, table - high).astype(BF16)
    square = (rows, rows)
    same = lax.broadcasted_iota(jnp.int32, square, 0) == lax.broadcasted_iota(jnp.int32, square, 1)
    out_ref[:, columns:] = against(jnp.where(same, 1.0, 0.0).astype(BF16), table).astype(BF16)


def make_payload(layer_in, route_ids, route_scores, owners):
    rows, columns = layer_in.shape
    extra = -(-2 * owners // LANES) * LANES
    return pl.pallas_call(
        functools.partial(payload_kernel, owners),
        out_shape=jax.ShapeDtypeStruct((rows, columns + extra), BF16),
        name="payload",
    )(layer_in, route_ids.T, route_scores.T)


def pre_kernel(x_ref, gate_ref, up_ref, out_ref):
    block = gate_ref.shape[0]
    out_ref[:, :block] = against(x_ref[...], gate_ref[...]).astype(out_ref.dtype)
    out_ref[:, block:] = against(x_ref[...], up_ref[...]).astype(out_ref.dtype)


def pre_parts(x, gate, up, dtype, name):
    hidden, columns = gate.shape
    rows, block = x.shape[0], block_of(hidden)
    return pl.pallas_call(
        pre_kernel,
        grid=(hidden // block,),
        in_specs=[
            pl.BlockSpec((rows, columns), lambda i: (0, 0)),
            pl.BlockSpec((block, columns), lambda i: (i, 0)),
            pl.BlockSpec((block, columns), lambda i: (i, 0)),
        ],
        out_specs=pl.BlockSpec((rows, 2 * block), lambda i: (0, i)),
        out_shape=jax.ShapeDtypeStruct((rows, 2 * hidden), dtype),
        compiler_params=params(),
        cost_estimate=cost(4 * rows * hidden * columns, 4 * hidden * columns + 4 * rows * hidden),
        name=name,
    )(x, gate, up)


def added(refs):
    total = refs[0][...].astype(F32)
    for ref in refs[1:]:
        total = total + ref[...].astype(F32)
    half = total.shape[1] // 2
    return total[:, :half], total[:, half:]


def teacher_kernel(parts, inner, owners, *refs):
    me_ref, pre_refs, down_ref, table_ref = refs[0], refs[1 : 1 + parts], refs[1 + parts], refs[2 + parts]
    out_refs, total = refs[3 + parts : 3 + parts + inner], refs[-1]
    step = pl.program_id(0)
    gate, up = added(pre_refs)
    hidden = (gate * jax.nn.sigmoid(gate) * up).astype(BF16)
    term = plain(hidden, down_ref[...])

    @pl.when(step == 0)
    def _():
        total[...] = term

    @pl.when(step > 0)
    def _():
        total[...] += term

    @pl.when(step == pl.num_programs(0) - 1)
    def _():
        me = me_ref[0]
        table = table_ref[...].astype(F32)
        lane = lax.broadcasted_iota(jnp.int32, table.shape, 1)
        mine = (lane == me) | (lane == me + owners)
        weight = jnp.sum(jnp.where(mine, table, 0.0), axis=1, keepdims=True)
        length = out_refs[0].shape[0]
        for k, out_ref in enumerate(out_refs):
            piece = slice(k * length, (k + 1) * length)
            out_ref[...] = (total[piece, :] * weight[piece, :]).astype(BF16)


def teacher_parts(me, pres, down, payload, inner, owners):
    hidden, columns = down.shape
    rows, block = payload.shape[0], block_of(hidden)
    extra = payload.shape[1] - columns
    return pl.pallas_call(
        functools.partial(teacher_kernel, len(pres), inner, owners),
        grid=(hidden // block,),
        in_specs=[pl.BlockSpec(memory_space=pltpu.SMEM)]
        + [pl.BlockSpec((rows, 2 * block), lambda i: (0, i)) for _ in pres]
        + [
            pl.BlockSpec((block, columns), lambda i: (i, 0)),
            pl.BlockSpec((rows, extra), lambda i: (0, columns // extra)),
        ],
        out_specs=[pl.BlockSpec((rows // inner, columns), lambda i: (0, 0)) for _ in range(inner)],
        out_shape=[jax.ShapeDtypeStruct((rows // inner, columns), BF16) for _ in range(inner)],
        scratch_shapes=[pltpu.VMEM((rows, columns), F32)],
        compiler_params=params(),
        cost_estimate=cost(2 * rows * hidden * columns, 2 * hidden * columns + 10 * rows * hidden),
        name="teacher_down",
    )(me, *pres, down, payload)


def student_kernel(parts, inner, *refs):
    pre_refs, down_ref, teacher_refs = refs[:parts], refs[parts], refs[parts + 1 : parts + 1 + inner]
    hidden_ref, out_refs, total = refs[parts + 1 + inner], refs[parts + 2 + inner : -1], refs[-1]
    step = pl.program_id(0)
    gate, up = added(pre_refs)
    hidden = (gate * jax.nn.sigmoid(gate) * up).astype(BF16)
    hidden_ref[...] = hidden
    term = plain(hidden, down_ref[...])

    @pl.when(step == 0)
    def _():
        total[...] = term

    @pl.when(step > 0)
    def _():
        total[...] += term

    @pl.when(step == pl.num_programs(0) - 1)
    def _():
        length = out_refs[0].shape[0]
        for k, out_ref in enumerate(out_refs):
            out_ref[...] = (total[k * length : (k + 1) * length, :] - teacher_refs[k][...].astype(F32)).astype(BF16)


def student_parts(pres, down, teacher):
    hidden, columns = down.shape
    rows, block, inner = pres[0].shape[0], block_of(hidden), len(teacher)
    whole = pl.BlockSpec((rows // inner, columns), lambda i: (0, 0))
    outs = pl.pallas_call(
        functools.partial(student_kernel, len(pres), inner),
        grid=(hidden // block,),
        in_specs=[pl.BlockSpec((rows, 2 * block), lambda i: (0, i)) for _ in pres]
        + [pl.BlockSpec((block, columns), lambda i: (i, 0))]
        + [whole] * inner,
        out_specs=[pl.BlockSpec((rows, block), lambda i: (0, i))] + [whole] * inner,
        out_shape=[jax.ShapeDtypeStruct((rows, hidden), BF16)]
        + [jax.ShapeDtypeStruct((rows // inner, columns), BF16) for _ in range(inner)],
        scratch_shapes=[pltpu.VMEM((rows, columns), F32)],
        compiler_params=params(),
        cost_estimate=cost(2 * rows * hidden * columns, 2 * hidden * columns + 10 * rows * hidden),
        name="student_down",
    )(*pres, down, *teacher)
    return outs[0], outs[1:]


def hidden_grad_kernel(delta_ref, down_ref, out_ref):
    out_ref[...] = against(delta_ref[...], down_ref[...]).astype(BF16)


def hidden_grad_parts(delta, down):
    hidden, columns = down.shape
    rows, block = delta.shape[0], block_of(hidden)
    return pl.pallas_call(
        hidden_grad_kernel,
        grid=(hidden // block,),
        in_specs=[
            pl.BlockSpec((rows, columns), lambda i: (0, 0)),
            pl.BlockSpec((block, columns), lambda i: (i, 0)),
        ],
        out_specs=pl.BlockSpec((rows, block), lambda i: (0, i)),
        out_shape=jax.ShapeDtypeStruct((rows, hidden), BF16),
        compiler_params=params(),
        cost_estimate=cost(2 * rows * hidden * columns, 2 * hidden * columns + 2 * rows * columns),
        name="hidden_grad",
    )(delta, down)


def grad_down_kernel(hidden_ref, delta_ref, out_ref):
    out_ref[...] = across(hidden_ref[...], delta_ref[...]).astype(BF16)


def grad_down_of(hidden_rows, delta):
    rows, hidden = hidden_rows.shape
    columns, block = delta.shape[1], block_of(hidden)
    return pl.pallas_call(
        grad_down_kernel,
        grid=(hidden // block,),
        in_specs=[
            pl.BlockSpec((rows, block), lambda i: (0, i)),
            pl.BlockSpec((rows, columns), lambda i: (0, 0)),
        ],
        out_specs=pl.BlockSpec((block, columns), lambda i: (i, 0)),
        out_shape=jax.ShapeDtypeStruct((hidden, columns), BF16),
        compiler_params=params(),
        cost_estimate=cost(2 * rows * hidden * columns, 2 * hidden * columns + 2 * rows * columns),
        name="grad_down",
    )(hidden_rows, delta)


def grad_pre_kernel(parts, *refs):
    pre_refs, back_refs, x_ref = refs[:parts], refs[parts : 2 * parts], refs[2 * parts]
    gate_ref, up_ref = refs[-2:]
    gate, up = added(pre_refs)
    back = back_refs[0][...].astype(F32)
    for ref in back_refs[1:]:
        back = back + ref[...].astype(F32)
    sig = jax.nn.sigmoid(gate)
    gate_grad = (back * up * sig * (1.0 + gate * (1.0 - sig))).astype(BF16)
    up_grad = (back * gate * sig).astype(BF16)
    gate_ref[...] = across(gate_grad, x_ref[...]).astype(BF16)
    up_ref[...] = across(up_grad, x_ref[...]).astype(BF16)


def grad_pre_of(pres, backs, payload, columns):
    rows, hidden = backs[0].shape
    block = block_of(hidden)
    return pl.pallas_call(
        functools.partial(grad_pre_kernel, len(pres)),
        grid=(hidden // block,),
        in_specs=[pl.BlockSpec((rows, 2 * block), lambda i: (0, i)) for _ in pres]
        + [pl.BlockSpec((rows, block), lambda i: (0, i)) for _ in backs]
        + [pl.BlockSpec((rows, columns), lambda i: (0, 0))],
        out_specs=[pl.BlockSpec((block, columns), lambda i: (i, 0))] * 2,
        out_shape=[jax.ShapeDtypeStruct((hidden, columns), BF16)] * 2,
        compiler_params=params(),
        cost_estimate=cost(4 * rows * hidden * columns, 4 * hidden * columns + 2 * rows * columns),
        name="grad_gate_up",
    )(*pres, *backs, payload)


def shards(
    layer_in,
    route_ids,
    route_scores,
    expert_gate,
    expert_up,
    expert_down,
    student_gate,
    student_up,
    student_down,
):
    owners = lax.axis_size("wide")
    ring = Ring(owners)
    tok_rows, columns = layer_in.shape
    me = lax.axis_index("wide").astype(jnp.int32).reshape(1)

    payload = ring.gather(make_payload(layer_in, route_ids, route_scores, owners))

    expert_pre = pre_parts(payload, expert_gate[0], expert_up[0], BF16, "teacher_pre")
    expert_pres = [expert_pre] + from_pair(expert_pre)
    student_pre = pre_parts(payload, student_gate, student_up, F32, "student_pre")
    student_pres = [student_pre] + from_pair(student_pre)
    teacher = teacher_parts(me, expert_pres, expert_down[0], payload, ring.inner, owners)
    student_hidden, difference = student_parts(student_pres, student_down, teacher)

    loss_scale = 1.0 / math.sqrt(tok_rows * owners)
    delta = (ring.reduce(difference) * loss_scale).astype(BF16)
    teacher_out = ring.reduce(teacher).astype(BF16)
    delta_all = ring.gather(delta)

    back = hidden_grad_parts(delta_all, student_down)
    backs = [back] + from_pair(back)
    grad_down = grad_down_of(student_hidden, delta_all)
    grad_gate, grad_up = grad_pre_of(student_pres, backs, payload, columns)
    return (teacher_out, grad_gate, grad_up, grad_down)


def solution(mesh):
    in_specs = (
        P("wide", "dp"),
        P("wide", None),
        P("wide", None),
        P("wide", None, "dp"),
        P("wide", None, "dp"),
        P("wide", None, "dp"),
        P("wide", "dp"),
        P("wide", "dp"),
        P("wide", "dp"),
    )
    out_specs = (P("wide", "dp"), P("wide", "dp"), P("wide", "dp"), P("wide", "dp"))
    return jax.shard_map(shards, mesh=mesh, in_specs=in_specs, out_specs=out_specs, check_vma=False)
```

```python
import functools
import math

import jax
import jax.numpy as jnp
from jax import lax
from jax.experimental import pallas as pl
from jax.experimental.pallas import tpu as pltpu
from jax.sharding import PartitionSpec as P

BF16 = jnp.bfloat16
F32 = jnp.float32
MIB = 1024 * 1024
LANES = 128
TEACHER_BLOCK = 768
STUDENT_BLOCK = 256


def against(left_mat, right_mat):
    return lax.dot_general(left_mat, right_mat, (((1,), (1,)), ((), ())), preferred_element_type=F32)


def across(left_mat, right_mat):
    return lax.dot_general(left_mat, right_mat, (((0,), (0,)), ((), ())), preferred_element_type=F32)


def plain(left_mat, right_mat):
    return lax.dot_general(left_mat, right_mat, (((1,), (0,)), ((), ())), preferred_element_type=F32)


def block_of(size, most=384):
    fits = [b for b in range(LANES, most + 1, LANES) if size % b == 0]
    return fits[-1] if fits else size


def params(rows):
    limit = min(18 * max(1, rows // 256), 56) * MIB
    return pltpu.CompilerParams(vmem_limit_bytes=limit, dimension_semantics=("arbitrary",))


def cost(flops, nbytes):
    return pl.CostEstimate(flops=int(flops), bytes_accessed=int(nbytes), transcendentals=0)


class Ring:
    def __init__(self, size):
        assert size & (size - 1) == 0 and size >= 4, size
        self.size, self.inner = size, 1 << (size.bit_length() - 1) // 2
        self.outer = size // self.inner

    def swap(self, value, near, far):
        flip = near + self.inner * far
        return lax.ppermute(value, "wide", [(i, i ^ flip) for i in range(self.size)])

    def gather_far(self, value):
        return [self.swap(value, 0, k) for k in range(1, self.outer)]

    def gather_near(self, value):
        return [self.swap(value, k, 0) for k in range(1, self.inner)]

    def joined(self, value, near, column, rest):
        blocks = [value, column]
        for first, others in zip(near, rest):
            blocks += [first, others]
        return jnp.concatenate(blocks, axis=0)

    def reduce_near(self, pieces):
        arrived = [pieces[0]] + [self.swap(pieces[k], k, 0) for k in range(1, self.inner)]
        return sum(a.astype(F32) for a in arrived).astype(BF16)

    def reduce_far(self, blocks):
        arrived = [blocks[0]] + [self.swap(blocks[k], 0, k) for k in range(1, self.outer)]
        return sum(a.astype(F32) for a in arrived)


def from_pair(value):
    size = lax.axis_size("dp")
    return [lax.ppermute(value, "dp", [(i, (i + s) % size) for i in range(size)]) for s in range(1, size)]


def payload_kernel(owners, layer_hbm, ids_hbm, scores_hbm, out_ref, ids_ref, scores_ref, sems):
    rows, columns = layer_hbm.shape
    copies = [
        pltpu.make_async_copy(ids_hbm, ids_ref, sems.at[0]),
        pltpu.make_async_copy(scores_hbm, scores_ref, sems.at[1]),
        pltpu.make_async_copy(layer_hbm, out_ref.at[:, pl.ds(0, columns)], sems.at[2]),
    ]
    for copy in copies:
        copy.start()
    copies[0].wait()
    copies[1].wait()
    scores = scores_ref[...]
    weights = scores / jnp.sum(scores, axis=0, keepdims=True)
    ids = ids_ref[...]
    shape = (out_ref.shape[1] - columns, rows)
    place = lax.broadcasted_iota(jnp.int32, shape, 0)
    expert = jnp.where(place >= owners, place - owners, place)
    table = jnp.zeros(shape, F32)
    for k in range(ids.shape[0]):
        table = table + jnp.where(ids[k : k + 1, :] == expert, weights[k : k + 1, :], 0.0)
    high = table.astype(BF16).astype(F32)
    table = jnp.where(place < owners, high, table - high)
    out_ref[:, columns:] = table.T.astype(BF16)
    copies[2].wait()


def make_payload(layer_in, route_ids, route_scores, owners):
    rows, columns = layer_in.shape
    extra = -(-2 * owners // LANES) * LANES
    return pl.pallas_call(
        functools.partial(payload_kernel, owners),
        in_specs=[pl.BlockSpec(memory_space=pltpu.HBM)] * 3,
        out_shape=jax.ShapeDtypeStruct((rows, columns + extra), BF16),
        scratch_shapes=[
            pltpu.VMEM(route_ids.shape[::-1], jnp.int32),
            pltpu.VMEM(route_scores.shape[::-1], F32),
            pltpu.SemaphoreType.DMA((3,)),
        ],
        compiler_params=pltpu.CompilerParams(vmem_limit_bytes=54 * MIB),
        name="payload",
    )(layer_in, route_ids.T, route_scores.T)


def pass_kernel(in_ref, out_ref):
    out_ref[...] = in_ref[...]


def passed(value):
    return pl.pallas_call(
        pass_kernel,
        out_shape=jax.ShapeDtypeStruct(value.shape, value.dtype),
        compiler_params=pltpu.CompilerParams(vmem_limit_bytes=2 * MIB),
        cost_estimate=cost(1e11, 1e5),
        name="passed",
    )(value)


def pre_kernel(x_ref, gate_ref, up_ref, out_ref):
    block = gate_ref.shape[0]
    out_ref[:, :block] = against(x_ref[...], gate_ref[...]).astype(out_ref.dtype)
    out_ref[:, block:] = against(x_ref[...], up_ref[...]).astype(out_ref.dtype)


def pre_parts(x, gate, up, dtype, most, name):
    hidden, columns = gate.shape
    rows, block = x.shape[0], block_of(hidden, most)
    return pl.pallas_call(
        pre_kernel,
        grid=(hidden // block,),
        in_specs=[
            pl.BlockSpec((rows, columns), lambda i: (0, 0)),
            pl.BlockSpec((block, columns), lambda i: (i, 0)),
            pl.BlockSpec((block, columns), lambda i: (i, 0)),
        ],
        out_specs=pl.BlockSpec((rows, 2 * block), lambda i: (0, i)),
        out_shape=jax.ShapeDtypeStruct((rows, 2 * hidden), dtype),
        compiler_params=params(rows),
        cost_estimate=cost(4 * rows * hidden * columns, 4 * hidden * columns + 4 * rows * hidden),
        name=name,
    )(x, gate, up)


def added(refs):
    total = refs[0][...].astype(F32)
    for ref in refs[1:]:
        total = total + ref[...].astype(F32)
    half = total.shape[1] // 2
    return total[:, :half], total[:, half:]


def teacher_places(rows, inner):
    length = rows // inner // 2
    for near in range(inner):
        for second in range(2):
            here = (2 * near + second) * length
            part = 2 + (near >> 1 & 1) if second else near & 1
            there = ((near >> 2) * 2 + (near & 1) if second else near >> 1) * length
            yield slice(here, here + length), near, part, slice(there, there + length)


def teacher_kernel(parts, inner, owners, *refs):
    pre_refs, down_ref, table_ref = refs[:parts], refs[parts], refs[parts + 1]
    out_refs, total = refs[parts + 2 : parts + 6], refs[-1]
    step = pl.program_id(0)
    gate, up = added(pre_refs)
    hidden = (gate * jax.nn.sigmoid(gate) * up).astype(BF16)
    term = plain(hidden, down_ref[...])

    @pl.when(step == 0)
    def _():
        total[...] = term

    @pl.when(step > 0)
    def _():
        total[...] += term

    @pl.when(step == pl.num_programs(0) - 1)
    def _():
        me = lax.axis_index("wide")
        table = table_ref[...].astype(F32)
        lane = lax.broadcasted_iota(jnp.int32, table.shape, 1)
        mine = (lane == me) | (lane == me + owners)
        weight = jnp.sum(jnp.where(mine, table, 0.0), axis=1, keepdims=True)
        for piece, _, part, place in teacher_places(total.shape[0], inner):
            out_refs[part][place, :] = (total[piece, :] * weight[piece, :]).astype(BF16)


def teacher_parts(pres, down, payload, inner, owners):
    hidden, columns = down.shape
    rows, block = payload.shape[0], block_of(hidden, TEACHER_BLOCK)
    extra = payload.shape[1] - columns
    return pl.pallas_call(
        functools.partial(teacher_kernel, len(pres), inner, owners),
        grid=(hidden // block,),
        in_specs=[pl.BlockSpec((rows, 2 * block), lambda i: (0, i)) for _ in pres]
        + [
            pl.BlockSpec((block, columns), lambda i: (i, 0)),
            pl.BlockSpec((rows, extra), lambda i: (0, columns // extra)),
        ],
        out_specs=[pl.BlockSpec((rows // 4, columns), lambda i: (0, 0))] * 4,
        out_shape=[jax.ShapeDtypeStruct((rows // 4, columns), BF16)] * 4,
        scratch_shapes=[pltpu.VMEM((rows, columns), F32)],
        compiler_params=params(rows),
        cost_estimate=cost(2 * rows * hidden * columns, 2 * hidden * columns + 10 * rows * hidden),
        name="teacher_down",
    )(*pres, down, payload)


def student_kernel(parts, inner, *refs):
    pre_refs, down_ref, teacher_refs = refs[:parts], refs[parts], refs[parts + 1 : parts + 5]
    hidden_ref, out_refs, total = refs[parts + 5], refs[parts + 6 : -1], refs[-1]
    step = pl.program_id(0)
    gate, up = added(pre_refs)
    hidden = (gate * jax.nn.sigmoid(gate) * up).astype(BF16)
    hidden_ref[...] = hidden
    term = plain(hidden, down_ref[...])

    @pl.when(step == 0)
    def _():
        total[...] = term

    @pl.when(step > 0)
    def _():
        total[...] += term

    @pl.when(step == pl.num_programs(0) - 1)
    def _():
        for piece, near, part, place in teacher_places(total.shape[0], inner):
            length = piece.stop - piece.start
            here = piece.start - 2 * near * length
            taught = teacher_refs[part][place, :].astype(F32)
            out_refs[near][here : here + length, :] = (total[piece, :] - taught).astype(BF16)


def student_parts(pres, down, teacher, inner):
    hidden, columns = down.shape
    rows, block = pres[0].shape[0], block_of(hidden, STUDENT_BLOCK)
    piece = (rows // inner, columns)
    outs = pl.pallas_call(
        functools.partial(student_kernel, len(pres), inner),
        grid=(hidden // block,),
        in_specs=[pl.BlockSpec((rows, 2 * block), lambda i: (0, i)) for _ in pres]
        + [pl.BlockSpec((block, columns), lambda i: (i, 0))]
        + [pl.BlockSpec((rows // 4, columns), lambda i: (0, 0))] * 4,
        out_specs=[pl.BlockSpec((rows, block), lambda i: (0, i))]
        + [pl.BlockSpec(piece, lambda i: (0, 0))] * inner,
        out_shape=[jax.ShapeDtypeStruct((rows, hidden), BF16)]
        + [jax.ShapeDtypeStruct(piece, BF16)] * inner,
        scratch_shapes=[pltpu.VMEM((rows, columns), F32)],
        compiler_params=params(rows),
        cost_estimate=cost(2 * rows * hidden * columns, 2 * hidden * columns + 10 * rows * hidden),
        name="student_down",
    )(*pres, down, *teacher)
    return outs[0], outs[1:]


def hidden_grad_kernel(delta_ref, down_ref, out_ref):
    out_ref[...] = against(delta_ref[...], down_ref[...]).astype(BF16)


def hidden_grad_parts(delta, down):
    hidden, columns = down.shape
    rows, block = delta.shape[0], block_of(hidden)
    return pl.pallas_call(
        hidden_grad_kernel,
        grid=(hidden // block,),
        in_specs=[
            pl.BlockSpec((rows, columns), lambda i: (0, 0)),
            pl.BlockSpec((block, columns), lambda i: (i, 0)),
        ],
        out_specs=pl.BlockSpec((rows, block), lambda i: (0, i)),
        out_shape=jax.ShapeDtypeStruct((rows, hidden), BF16),
        compiler_params=params(rows),
        cost_estimate=cost(2 * rows * hidden * columns, 2 * hidden * columns + 2 * rows * columns),
        name="hidden_grad",
    )(delta, down)


def grad_down_kernel(hidden_ref, delta_ref, out_ref):
    out_ref[...] = across(hidden_ref[...], delta_ref[...]).astype(BF16)


def grad_down_of(hidden_rows, delta):
    rows, hidden = hidden_rows.shape
    columns, block = delta.shape[1], block_of(hidden)
    return pl.pallas_call(
        grad_down_kernel,
        grid=(hidden // block,),
        in_specs=[
            pl.BlockSpec((rows, block), lambda i: (0, i)),
            pl.BlockSpec((rows, columns), lambda i: (0, 0)),
        ],
        out_specs=pl.BlockSpec((block, columns), lambda i: (i, 0)),
        out_shape=jax.ShapeDtypeStruct((hidden, columns), BF16),
        compiler_params=params(rows),
        cost_estimate=cost(2 * rows * hidden * columns, 2 * hidden * columns + 2 * rows * columns),
        name="grad_down",
    )(hidden_rows, delta)


def grad_pre_kernel(parts, *refs):
    pre_refs, back_refs, x_ref = refs[:parts], refs[parts : 2 * parts], refs[2 * parts]
    gate_ref, up_ref = refs[-2:]
    gate, up = added(pre_refs)
    back = back_refs[0][...].astype(F32)
    for ref in back_refs[1:]:
        back = back + ref[...].astype(F32)
    sig = jax.nn.sigmoid(gate)
    gate_grad = (back * up * sig * (1.0 + gate * (1.0 - sig))).astype(BF16)
    up_grad = (back * gate * sig).astype(BF16)
    gate_ref[...] = across(gate_grad, x_ref[...]).astype(BF16)
    up_ref[...] = across(up_grad, x_ref[...]).astype(BF16)


def grad_pre_of(pres, backs, payload, columns):
    rows, hidden = backs[0].shape
    block = block_of(hidden, STUDENT_BLOCK)
    return pl.pallas_call(
        functools.partial(grad_pre_kernel, len(pres)),
        grid=(hidden // block,),
        in_specs=[pl.BlockSpec((rows, 2 * block), lambda i: (0, i)) for _ in pres]
        + [pl.BlockSpec((rows, block), lambda i: (0, i)) for _ in backs]
        + [pl.BlockSpec((rows, columns), lambda i: (0, 0))],
        out_specs=[pl.BlockSpec((block, columns), lambda i: (i, 0))] * 2,
        out_shape=[jax.ShapeDtypeStruct((hidden, columns), BF16)] * 2,
        compiler_params=params(rows),
        cost_estimate=cost(4 * rows * hidden * columns, 4 * hidden * columns + 2 * rows * columns),
        name="grad_gate_up",
    )(*pres, *backs, payload)


def added_rows(one, other):
    return (one.astype(F32) + other.astype(F32)).astype(BF16)


def even_blocks(value, count):
    return value.reshape(count // 2, 2, -1, value.shape[1])[:, 0].reshape(-1, value.shape[1])


def odd_blocks(value, count):
    return value.reshape(count // 2, 2, -1, value.shape[1])[:, 1].reshape(-1, value.shape[1])


def shards(
    layer_in,
    route_ids,
    route_scores,
    expert_gate,
    expert_up,
    expert_down,
    student_gate,
    student_up,
    student_down,
):
    owners = lax.axis_size("wide")
    ring = Ring(owners)
    tok_rows, columns = layer_in.shape

    payload = make_payload(layer_in, route_ids, route_scores, owners)
    far = ring.gather_far(payload)
    far[0] = passed(far[0])
    far[0], payload = lax.optimization_barrier((far[0], payload))
    near = ring.gather_near(payload)
    column = jnp.concatenate(far, axis=0)
    rows = ring.joined(payload, near, column, ring.gather_near(column))

    expert_pre = pre_parts(rows, expert_gate[0], expert_up[0], BF16, TEACHER_BLOCK, "teacher_pre")
    expert_pres = [expert_pre] + from_pair(expert_pre)
    student_pre = pre_parts(rows, student_gate, student_up, F32, STUDENT_BLOCK, "student_pre")
    student_pres = [student_pre] + from_pair(student_pre)
    teacher = teacher_parts(expert_pres, expert_down[0], rows, ring.inner, owners)
    student_hidden, pieces = student_parts(student_pres, student_down, teacher, ring.inner)

    loss_scale = 1.0 / math.sqrt(tok_rows * owners)
    column, teacher = lax.optimization_barrier((ring.reduce_near(pieces), teacher))
    taught = [added_rows(teacher[2 * k], ring.swap(teacher[2 * k + 1], 1 + k, 0)) for k in range(2)]
    blocks = list(column.reshape(ring.outer, tok_rows, columns))
    blocks[0], taught = lax.optimization_barrier((blocks[0], taught))
    delta = (ring.reduce_far(blocks) * loss_scale).astype(BF16)

    column = jnp.concatenate([delta] + ring.gather_far(delta), axis=0)
    count = ring.inner // 2
    kept, sent = [even_blocks(t, count) for t in taught], [odd_blocks(t, count) for t in taught]
    column, kept = lax.optimization_barrier((column, kept))
    taught = [added_rows(kept[k], ring.swap(sent[k], 2 - k, 0)) for k in range(2)]
    bit = 4
    while bit < ring.inner:
        count //= 2
        taught = [added_rows(even_blocks(t, count), ring.swap(odd_blocks(t, count), bit, 0)) for t in taught]
        bit *= 2

    delta_all = jnp.concatenate([column] + ring.gather_near(column), axis=0)
    taught = jnp.concatenate(taught, axis=0).reshape(ring.outer, tok_rows, columns)
    blocks = list(taught)
    delta_all, blocks[0] = lax.optimization_barrier((delta_all, blocks[0]))
    teacher_out = ring.reduce_far(blocks).astype(BF16)

    back = hidden_grad_parts(delta_all, student_down)
    backs = [back] + from_pair(back)
    grad_down = grad_down_of(student_hidden, delta_all)
    grad_gate, grad_up = grad_pre_of(student_pres, backs, rows, columns)
    return (teacher_out, grad_gate, grad_up, grad_down)


def solution(mesh):
    in_specs = (
        P("wide", "dp"),
        P("wide", None),
        P("wide", None),
        P("wide", None, "dp"),
        P("wide", None, "dp"),
        P("wide", None, "dp"),
        P("wide", "dp"),
        P("wide", "dp"),
        P("wide", "dp"),
    )
    out_specs = (P("wide", "dp"), P("wide", "dp"), P("wide", "dp"), P("wide", "dp"))
    return jax.shard_map(shards, mesh=mesh, in_specs=in_specs, out_specs=out_specs, check_vma=False)
```

```python
import functools
import math

import jax
import jax.numpy as jnp
from jax import lax
from jax.experimental import pallas as pl
from jax.experimental.pallas import tpu as pltpu
from jax.sharding import PartitionSpec as P

BF16 = jnp.bfloat16
F32 = jnp.float32
MIB = 1024 * 1024
IN_VMEM = pl.BlockSpec(memory_space=pltpu.VMEM)
IN_HBM = pl.BlockSpec(memory_space=pltpu.HBM)
LANES = 128
TEACHER_BLOCK = 768
STUDENT_BLOCK = 256


def against(left_mat, right_mat):
    return lax.dot_general(left_mat, right_mat, (((1,), (1,)), ((), ())), preferred_element_type=F32)


def across(left_mat, right_mat):
    return lax.dot_general(left_mat, right_mat, (((0,), (0,)), ((), ())), preferred_element_type=F32)


def plain(left_mat, right_mat):
    return lax.dot_general(left_mat, right_mat, (((1,), (0,)), ((), ())), preferred_element_type=F32)


def block_of(size, most=384):
    fits = [b for b in range(LANES, most + 1, LANES) if size % b == 0]
    return fits[-1] if fits else size


def params(rows):
    limit = min(18 * max(1, rows // 256), 56) * MIB
    return pltpu.CompilerParams(vmem_limit_bytes=limit)


def cost(flops, nbytes):
    return pl.CostEstimate(flops=int(flops), bytes_accessed=int(nbytes), transcendentals=0)


class Ring:
    def __init__(self, size):
        assert size & (size - 1) == 0 and size >= 4, size
        self.size, self.inner = size, 1 << (size.bit_length() - 1) // 2
        self.outer = size // self.inner

    def swap(self, value, near, far):
        flip = near + self.inner * far
        return lax.ppermute(value, "wide", [(i, i ^ flip) for i in range(self.size)])

    def gather_far(self, value):
        return [self.swap(value, 0, k) for k in range(1, self.outer)]

    def gather_far_last(self, value):
        return [self.swap(value, 0, k) for k in range(self.outer - 1, 0, -1)][::-1]

    def gather_near(self, value):
        return [self.swap(value, k, 0) for k in range(1, self.inner)]

    def joined(self, value, near, column, rest):
        blocks = [value, column]
        for first, others in zip(near, rest):
            blocks += [first, others]
        return jnp.concatenate(blocks, axis=0)

    def reduce_near(self, pieces):
        arrived = [pieces[0]] + [self.swap(pieces[k], k, 0) for k in range(1, self.inner)]
        return sum(a.astype(F32) for a in arrived).astype(BF16)

    def reduce_far(self, blocks):
        arrived = [blocks[0]] + [self.swap(blocks[k], 0, k) for k in range(1, self.outer)]
        return sum(a.astype(F32) for a in arrived)


def from_pair(value):
    size = lax.axis_size("dp")
    return [lax.ppermute(value, "dp", [(i, (i + s) % size) for i in range(size)]) for s in range(1, size)]


def payload_kernel(owners, layer_hbm, ids_hbm, scores_hbm, out_ref, ids_ref, scores_ref, sems):
    rows, columns = layer_hbm.shape
    copies = [
        pltpu.make_async_copy(ids_hbm, ids_ref, sems.at[0]),
        pltpu.make_async_copy(scores_hbm, scores_ref, sems.at[1]),
        pltpu.make_async_copy(layer_hbm, out_ref.at[:, pl.ds(0, columns)], sems.at[2]),
    ]
    for copy in copies:
        copy.start()
    copies[0].wait()
    copies[1].wait()
    scores = scores_ref[...]
    weights = scores / jnp.sum(scores, axis=0, keepdims=True)
    ids = ids_ref[...]
    shape = (out_ref.shape[1] - columns, rows)
    place = lax.broadcasted_iota(jnp.int32, shape, 0)
    expert = jnp.where(place >= owners, place - owners, place)
    table = jnp.zeros(shape, F32)
    for k in range(ids.shape[0]):
        table = table + jnp.where(ids[k : k + 1, :] == expert, weights[k : k + 1, :], 0.0)
    high = table.astype(BF16).astype(F32)
    table = jnp.where(place < owners, high, table - high)
    out_ref[:, columns:] = table.T.astype(BF16)
    copies[2].wait()


def make_payload(layer_in, route_ids, route_scores, owners):
    rows, columns = layer_in.shape
    extra = -(-2 * owners // LANES) * LANES
    return pl.pallas_call(
        functools.partial(payload_kernel, owners),
        in_specs=[IN_HBM] * 3,
        out_shape=jax.ShapeDtypeStruct((rows, columns + extra), BF16),
        scratch_shapes=[
            pltpu.VMEM(route_ids.shape[::-1], jnp.int32),
            pltpu.VMEM(route_scores.shape[::-1], F32),
            pltpu.SemaphoreType.DMA((3,)),
        ],
        compiler_params=pltpu.CompilerParams(vmem_limit_bytes=54 * MIB),
        name="payload",
    )(layer_in, route_ids.T, route_scores.T)


def pass_kernel(in_ref, out_ref):
    out_ref[...] = in_ref[...]


def passed(value):
    return pl.pallas_call(
        pass_kernel,
        out_shape=jax.ShapeDtypeStruct(value.shape, value.dtype),
        compiler_params=pltpu.CompilerParams(vmem_limit_bytes=2 * MIB),
        cost_estimate=cost(1e11, 1e5),
        name="passed",
    )(value)


def pre_kernel(block, x_ref, gate_ref, up_ref, out_ref):
    columns = gate_ref.shape[1]
    for i in range(gate_ref.shape[0] // block):
        here = slice(i * block, (i + 1) * block)
        for k, mat_ref in enumerate((gate_ref, up_ref)):
            there = slice((2 * i + k) * block, (2 * i + k + 1) * block)
            out_ref[:, there] = against(x_ref[:, :columns], mat_ref[here, :]).astype(out_ref.dtype)


def pre_parts(x, gate, up, dtype, most, name):
    hidden, columns = gate.shape
    rows, block = x.shape[0], block_of(hidden, most)
    return pl.pallas_call(
        functools.partial(pre_kernel, block),
        in_specs=[IN_VMEM] * 3,
        out_specs=IN_VMEM,
        out_shape=jax.ShapeDtypeStruct((rows, 2 * hidden), dtype),
        compiler_params=params(rows),
        cost_estimate=cost(4 * rows * hidden * columns, 4 * hidden * columns + 4 * rows * hidden),
        name=name,
    )(x, gate, up)


def added(refs, block, i):
    here = slice(2 * i * block, 2 * (i + 1) * block)
    total = refs[0][:, here].astype(F32)
    for ref in refs[1:]:
        total = total + ref[:, here].astype(F32)
    return total[:, :block], total[:, block:]


def activated(refs, block, i):
    gate, up = added(refs, block, i)
    return (gate * jax.nn.sigmoid(gate) * up).astype(BF16)


def teacher_places(rows, inner):
    length = rows // inner // 2
    for near in range(inner):
        for second in range(2):
            here = (2 * near + second) * length
            part = 2 + (near >> 1 & 1) if second else near & 1
            there = ((near >> 2) * 2 + (near & 1) if second else near >> 1) * length
            yield slice(here, here + length), near, part, slice(there, there + length)


def teacher_kernel(parts, inner, owners, block, *refs):
    pre_refs, down_ref, table_ref = refs[:parts], refs[parts], refs[parts + 1]
    out_refs, total = refs[parts + 2 : parts + 6], refs[-1]
    extra = table_ref.shape[1] - down_ref.shape[1]
    for i in range(down_ref.shape[0] // block):
        term = plain(activated(pre_refs, block, i), down_ref[i * block : (i + 1) * block, :])
        if i == 0:
            total[...] = term
        else:
            total[...] += term
    me = lax.axis_index("wide")
    table = table_ref[:, down_ref.shape[1] :].astype(F32)
    lane = lax.broadcasted_iota(jnp.int32, (table.shape[0], extra), 1)
    mine = (lane == me) | (lane == me + owners)
    weight = jnp.sum(jnp.where(mine, table, 0.0), axis=1, keepdims=True)
    for piece, _, part, place in teacher_places(total.shape[0], inner):
        out_refs[part][place, :] = (total[piece, :] * weight[piece, :]).astype(BF16)


def teacher_parts(pres, down, payload, inner, owners):
    hidden, columns = down.shape
    rows, block = payload.shape[0], block_of(hidden, TEACHER_BLOCK)
    return pl.pallas_call(
        functools.partial(teacher_kernel, len(pres), inner, owners, block),
        in_specs=[IN_VMEM] * (len(pres) + 2),
        out_specs=[IN_VMEM] * 4,
        out_shape=[jax.ShapeDtypeStruct((rows // 4, columns), BF16)] * 4,
        scratch_shapes=[pltpu.VMEM((rows, columns), F32)],
        compiler_params=params(rows),
        cost_estimate=cost(2 * rows * hidden * columns, 2 * hidden * columns + 10 * rows * hidden),
        name="teacher_down",
    )(*pres, down, payload)


def student_kernel(parts, inner, block, *refs):
    pre_refs, down_ref, teacher_refs = refs[:parts], refs[parts], refs[parts + 1 : parts + 5]
    hidden_ref, out_refs, total = refs[parts + 5], refs[parts + 6 : -1], refs[-1]
    for i in range(down_ref.shape[0] // block):
        here = slice(i * block, (i + 1) * block)
        hidden = activated(pre_refs, block, i)
        hidden_ref[:, here] = hidden
        term = plain(hidden, down_ref[here, :])
        if i == 0:
            total[...] = term
        else:
            total[...] += term
    for piece, near, part, place in teacher_places(total.shape[0], inner):
        length = piece.stop - piece.start
        here = piece.start - 2 * near * length
        taught = teacher_refs[part][place, :].astype(F32)
        out_refs[near][here : here + length, :] = (total[piece, :] - taught).astype(BF16)


def student_parts(pres, down, teacher, inner):
    hidden, columns = down.shape
    rows, block = pres[0].shape[0], block_of(hidden, STUDENT_BLOCK)
    outs = pl.pallas_call(
        functools.partial(student_kernel, len(pres), inner, block),
        in_specs=[IN_VMEM] * (len(pres) + 5),
        out_specs=[IN_VMEM] * (1 + inner),
        out_shape=[jax.ShapeDtypeStruct((rows, hidden), BF16)]
        + [jax.ShapeDtypeStruct((rows // inner, columns), BF16)] * inner,
        scratch_shapes=[pltpu.VMEM((rows, columns), F32)],
        compiler_params=params(rows),
        cost_estimate=cost(2 * rows * hidden * columns, 2 * hidden * columns + 10 * rows * hidden),
        name="student_down",
    )(*pres, down, *teacher)
    return outs[0], outs[1:]


def hidden_grad_kernel(block, delta_ref, down_ref, out_ref):
    for i in range(out_ref.shape[1] // block):
        here = slice(i * block, (i + 1) * block)
        out_ref[:, here] = against(delta_ref[...], down_ref[here, :]).astype(BF16)


def hidden_grad_parts(delta, down):
    hidden, columns = down.shape
    rows = delta.shape[0]
    return pl.pallas_call(
        functools.partial(hidden_grad_kernel, block_of(hidden)),
        in_specs=[IN_VMEM] * 2,
        out_specs=IN_VMEM,
        out_shape=jax.ShapeDtypeStruct((rows, hidden), BF16),
        compiler_params=params(rows),
        cost_estimate=cost(2 * rows * hidden * columns, 2 * hidden * columns + 2 * rows * columns),
        name="hidden_grad",
    )(delta, down)


def grad_down_kernel(block, hidden_ref, delta_ref, out_hbm, out_ref, sems):
    copies = []
    for i in range(out_hbm.shape[0] // block):
        here = slice(i * block, (i + 1) * block)
        out_ref[here, :] = across(hidden_ref[:, here], delta_ref[...]).astype(BF16)
        copies.append(pltpu.make_async_copy(out_ref.at[here, :], out_hbm.at[here, :], sems.at[i]))
        copies[-1].start()
    for copy in copies:
        copy.wait()


def grad_down_of(hidden_rows, delta):
    rows, hidden = hidden_rows.shape
    columns, block = delta.shape[1], block_of(hidden, 256)
    return pl.pallas_call(
        functools.partial(grad_down_kernel, block),
        in_specs=[IN_VMEM] * 2,
        out_specs=IN_HBM,
        out_shape=jax.ShapeDtypeStruct((hidden, columns), BF16),
        scratch_shapes=[pltpu.VMEM((hidden, columns), BF16), pltpu.SemaphoreType.DMA((hidden // block,))],
        compiler_params=params(rows),
        cost_estimate=cost(2 * rows * hidden * columns, 2 * hidden * columns + 2 * rows * columns),
        name="grad_down",
    )(hidden_rows, delta)


def grad_pre_kernel(parts, block, *refs):
    pre_refs, back_refs, x_ref = refs[:parts], refs[parts : 2 * parts], refs[2 * parts]
    outs_hbm, out_refs, sems = refs[2 * parts + 1 : 2 * parts + 3], refs[-3:-1], refs[-1]
    columns = outs_hbm[0].shape[1]
    copies = []
    for i in range(outs_hbm[0].shape[0] // block):
        here = slice(i * block, (i + 1) * block)
        gate, up = added(pre_refs, block, i)
        back = back_refs[0][:, here].astype(F32)
        for ref in back_refs[1:]:
            back = back + ref[:, here].astype(F32)
        sig = jax.nn.sigmoid(gate)
        grads = (back * up * sig * (1.0 + gate * (1.0 - sig))).astype(BF16), (back * gate * sig).astype(BF16)
        for k in range(2):
            out_refs[k][here, :] = across(grads[k], x_ref[:, :columns]).astype(BF16)
            copies.append(pltpu.make_async_copy(out_refs[k].at[here, :], outs_hbm[k].at[here, :], sems.at[k, i]))
            copies[-1].start()
    for copy in copies:
        copy.wait()


def grad_pre_of(pres, backs, payload, columns):
    rows, hidden = backs[0].shape
    block = block_of(hidden, STUDENT_BLOCK)
    return pl.pallas_call(
        functools.partial(grad_pre_kernel, len(pres), block),
        in_specs=[IN_VMEM] * (2 * len(pres) + 1),
        out_specs=[IN_HBM] * 2,
        out_shape=[jax.ShapeDtypeStruct((hidden, columns), BF16)] * 2,
        scratch_shapes=[pltpu.VMEM((hidden, columns), BF16)] * 2 + [pltpu.SemaphoreType.DMA((2, hidden // block))],
        compiler_params=params(rows),
        cost_estimate=cost(4 * rows * hidden * columns, 4 * hidden * columns + 2 * rows * columns),
        name="grad_gate_up",
    )(*pres, *backs, payload)


def added_rows(one, other):
    return (one.astype(F32) + other.astype(F32)).astype(BF16)


def even_blocks(value, count):
    return value.reshape(count // 2, 2, -1, value.shape[1])[:, 0].reshape(-1, value.shape[1])


def odd_blocks(value, count):
    return value.reshape(count // 2, 2, -1, value.shape[1])[:, 1].reshape(-1, value.shape[1])


def shards(
    layer_in,
    route_ids,
    route_scores,
    expert_gate,
    expert_up,
    expert_down,
    student_gate,
    student_up,
    student_down,
):
    owners = lax.axis_size("wide")
    ring = Ring(owners)
    tok_rows, columns = layer_in.shape

    payload = make_payload(layer_in, route_ids, route_scores, owners)
    far = ring.gather_far_last(payload)
    far[-1] = passed(far[-1])
    far[-1], payload = lax.optimization_barrier((far[-1], payload))
    near = ring.gather_near(payload)
    column = jnp.concatenate(far, axis=0)
    rows = ring.joined(payload, near, column, ring.gather_near(column))

    expert_pre = pre_parts(rows, expert_gate[0], expert_up[0], BF16, TEACHER_BLOCK, "teacher_pre")
    expert_pres = [expert_pre] + from_pair(expert_pre)
    student_pre = pre_parts(rows, student_gate, student_up, F32, STUDENT_BLOCK, "student_pre")
    student_pres = [student_pre] + from_pair(student_pre)
    teacher = teacher_parts(expert_pres, expert_down[0], rows, ring.inner, owners)
    student_hidden, pieces = student_parts(student_pres, student_down, teacher, ring.inner)

    loss_scale = 1.0 / math.sqrt(tok_rows * owners)
    column, teacher = lax.optimization_barrier((ring.reduce_near(pieces), teacher))
    taught = [added_rows(teacher[2 * k], ring.swap(teacher[2 * k + 1], 1 + k, 0)) for k in range(2)]
    blocks = list(column.reshape(ring.outer, tok_rows, columns))
    blocks[0], taught = lax.optimization_barrier((blocks[0], taught))
    delta = (ring.reduce_far(blocks) * loss_scale).astype(BF16)

    column = jnp.concatenate([delta] + ring.gather_far(delta), axis=0)
    count = ring.inner // 2
    kept, sent = [even_blocks(t, count) for t in taught], [odd_blocks(t, count) for t in taught]
    column, kept = lax.optimization_barrier((column, kept))
    taught = lax.optimization_barrier([added_rows(kept[k], ring.swap(sent[k], 2 - k, 0)) for k in range(2)])
    bit = 4
    while bit < ring.inner:
        count //= 2
        taught = [added_rows(even_blocks(t, count), ring.swap(odd_blocks(t, count), bit, 0)) for t in taught]
        bit *= 2

    delta_all = jnp.concatenate([column] + ring.gather_near(column), axis=0)
    taught = jnp.concatenate(taught, axis=0).reshape(ring.outer, tok_rows, columns)
    blocks = list(taught)
    delta_all, blocks[0] = lax.optimization_barrier((delta_all, blocks[0]))
    teacher_out = ring.reduce_far(blocks).astype(BF16)

    back = hidden_grad_parts(delta_all, student_down)
    backs = [back] + from_pair(back)
    grad_down = grad_down_of(student_hidden, delta_all)
    grad_gate, grad_up = grad_pre_of(student_pres, backs, rows, columns)
    return (teacher_out, grad_gate, grad_up, grad_down)


def solution(mesh):
    in_specs = (
        P("wide", "dp"),
        P("wide", None),
        P("wide", None),
        P("wide", None, "dp"),
        P("wide", None, "dp"),
        P("wide", None, "dp"),
        P("wide", "dp"),
        P("wide", "dp"),
        P("wide", "dp"),
    )
    out_specs = (P("wide", "dp"), P("wide", "dp"), P("wide", "dp"), P("wide", "dp"))
    return jax.shard_map(shards, mesh=mesh, in_specs=in_specs, out_specs=out_specs, check_vma=False)
```

```python
import functools
import math

import jax
import jax.numpy as jnp
from jax import lax
from jax.experimental import pallas as pl
from jax.experimental.pallas import tpu as pltpu
from jax.sharding import PartitionSpec as P

BF16 = jnp.bfloat16
F32 = jnp.float32
MIB = 1024 * 1024
IN_VMEM = pl.BlockSpec(memory_space=pltpu.VMEM)
IN_HBM = pl.BlockSpec(memory_space=pltpu.HBM)
LANES = 128
TEACHER_BLOCK = 768
STUDENT_BLOCK = 256


def against(left_mat, right_mat):
    return lax.dot_general(left_mat, right_mat, (((1,), (1,)), ((), ())), preferred_element_type=F32)


def across(left_mat, right_mat):
    return lax.dot_general(left_mat, right_mat, (((0,), (0,)), ((), ())), preferred_element_type=F32)


def plain(left_mat, right_mat):
    return lax.dot_general(left_mat, right_mat, (((1,), (0,)), ((), ())), preferred_element_type=F32)


def block_of(size, most=384):
    fits = [b for b in range(LANES, most + 1, LANES) if size % b == 0]
    return fits[-1] if fits else size


def params(rows):
    limit = min(18 * max(1, rows // 256), 56) * MIB
    return pltpu.CompilerParams(vmem_limit_bytes=limit)


def cost(flops, nbytes):
    return pl.CostEstimate(flops=int(flops), bytes_accessed=int(nbytes), transcendentals=0)


class Ring:
    def __init__(self, size):
        assert size & (size - 1) == 0 and size >= 4, size
        self.size, self.inner = size, 1 << (size.bit_length() - 1) // 2
        self.outer = size // self.inner

    def swap(self, value, near, far):
        flip = near + self.inner * far
        return lax.ppermute(value, "wide", [(i, i ^ flip) for i in range(self.size)])

    def gather_far(self, value):
        return [self.swap(value, 0, k) for k in range(1, self.outer)]

    def gather_far_last(self, value):
        return [self.swap(value, 0, k) for k in range(self.outer - 1, 0, -1)][::-1]

    def gather_near(self, value):
        return [self.swap(value, k, 0) for k in range(1, self.inner)]

    def joined(self, value, near, column, rest):
        blocks = [value, column]
        for first, others in zip(near, rest):
            blocks += [first, others]
        return jnp.concatenate(blocks, axis=0)

    def reduce_near(self, pieces):
        arrived = [pieces[0]] + [self.swap(pieces[k], k, 0) for k in range(1, self.inner)]
        return sum(a.astype(F32) for a in arrived).astype(BF16)

    def reduce_far(self, blocks):
        return [blocks[0]] + [self.swap(blocks[k], 0, k) for k in range(1, self.outer)]


def from_pair(value):
    size = lax.axis_size("dp")
    return [lax.ppermute(value, "dp", [(i, (i + s) % size) for i in range(size)]) for s in range(1, size)]


def payload_kernel(owners, layer_hbm, ids_hbm, scores_hbm, out_ref, ids_ref, scores_ref, sems):
    rows, columns = layer_hbm.shape
    copies = [
        pltpu.make_async_copy(ids_hbm, ids_ref, sems.at[0]),
        pltpu.make_async_copy(scores_hbm, scores_ref, sems.at[1]),
        pltpu.make_async_copy(layer_hbm, out_ref.at[:, pl.ds(0, columns)], sems.at[2]),
    ]
    for copy in copies:
        copy.start()
    copies[0].wait()
    copies[1].wait()
    scores = scores_ref[...]
    weights = scores / jnp.sum(scores, axis=0, keepdims=True)
    ids = ids_ref[...]
    shape = (out_ref.shape[1] - columns, rows)
    place = lax.broadcasted_iota(jnp.int32, shape, 0)
    expert = jnp.where(place >= owners, place - owners, place)
    table = jnp.zeros(shape, F32)
    for k in range(ids.shape[0]):
        table = table + jnp.where(ids[k : k + 1, :] == expert, weights[k : k + 1, :], 0.0)
    high = table.astype(BF16).astype(F32)
    table = jnp.where(place < owners, high, table - high)
    out_ref[:, columns:] = table.T.astype(BF16)
    copies[2].wait()


def make_payload(layer_in, route_ids, route_scores, owners):
    rows, columns = layer_in.shape
    extra = -(-2 * owners // LANES) * LANES
    return pl.pallas_call(
        functools.partial(payload_kernel, owners),
        in_specs=[IN_HBM] * 3,
        out_shape=jax.ShapeDtypeStruct((rows, columns + extra), BF16),
        scratch_shapes=[
            pltpu.VMEM(route_ids.shape[::-1], jnp.int32),
            pltpu.VMEM(route_scores.shape[::-1], F32),
            pltpu.SemaphoreType.DMA((3,)),
        ],
        compiler_params=pltpu.CompilerParams(vmem_limit_bytes=54 * MIB),
        name="payload",
    )(layer_in, route_ids.T, route_scores.T)


def pass_kernel(in_ref, out_ref):
    out_ref[...] = in_ref[...]


def passed(value):
    return pl.pallas_call(
        pass_kernel,
        out_shape=jax.ShapeDtypeStruct(value.shape, value.dtype),
        compiler_params=pltpu.CompilerParams(vmem_limit_bytes=2 * MIB),
        cost_estimate=cost(1e11, 1e5),
        name="passed",
    )(value)


def pre_kernel(block, x_ref, gate_ref, up_ref, out_ref):
    columns = gate_ref.shape[1]
    for i in range(gate_ref.shape[0] // block):
        here = slice(i * block, (i + 1) * block)
        for k, mat_ref in enumerate((gate_ref, up_ref)):
            there = slice((2 * i + k) * block, (2 * i + k + 1) * block)
            out_ref[:, there] = against(x_ref[:, :columns], mat_ref[here, :]).astype(out_ref.dtype)


def pre_parts(x, gate, up, dtype, most, name):
    hidden, columns = gate.shape
    rows, block = x.shape[0], block_of(hidden, most)
    return pl.pallas_call(
        functools.partial(pre_kernel, block),
        in_specs=[IN_VMEM] * 3,
        out_specs=IN_VMEM,
        out_shape=jax.ShapeDtypeStruct((rows, 2 * hidden), dtype),
        compiler_params=params(rows),
        cost_estimate=cost(4 * rows * hidden * columns, 4 * hidden * columns + 4 * rows * hidden),
        name=name,
    )(x, gate, up)


def added(refs, block, i):
    here = slice(2 * i * block, 2 * (i + 1) * block)
    total = refs[0][:, here].astype(F32)
    for ref in refs[1:]:
        total = total + ref[:, here].astype(F32)
    return total[:, :block], total[:, block:]


def activated(refs, block, i):
    gate, up = added(refs, block, i)
    return (gate * jax.nn.sigmoid(gate) * up).astype(BF16)


def teacher_places(rows, inner):
    length = rows // inner // 2
    for near in range(inner):
        for second in range(2):
            here = (2 * near + second) * length
            part = 2 + (near >> 1 & 1) if second else near & 1
            there = ((near >> 2) * 2 + (near & 1) if second else near >> 1) * length
            yield slice(here, here + length), near, part, slice(there, there + length)


def teacher_kernel(parts, inner, owners, block, *refs):
    pre_refs, down_ref, table_ref = refs[:parts], refs[parts], refs[parts + 1]
    out_refs, total = refs[parts + 2 : parts + 6], refs[-1]
    extra = table_ref.shape[1] - down_ref.shape[1]
    for i in range(down_ref.shape[0] // block):
        term = plain(activated(pre_refs, block, i), down_ref[i * block : (i + 1) * block, :])
        if i == 0:
            total[...] = term
        else:
            total[...] += term
    me = lax.axis_index("wide")
    table = table_ref[:, down_ref.shape[1] :].astype(F32)
    lane = lax.broadcasted_iota(jnp.int32, (table.shape[0], extra), 1)
    mine = (lane == me) | (lane == me + owners)
    weight = jnp.sum(jnp.where(mine, table, 0.0), axis=1, keepdims=True)
    for piece, _, part, place in teacher_places(total.shape[0], inner):
        out_refs[part][place, :] = (total[piece, :] * weight[piece, :]).astype(BF16)


def teacher_parts(pres, down, payload, inner, owners):
    hidden, columns = down.shape
    rows, block = payload.shape[0], block_of(hidden, TEACHER_BLOCK)
    return pl.pallas_call(
        functools.partial(teacher_kernel, len(pres), inner, owners, block),
        in_specs=[IN_VMEM] * (len(pres) + 2),
        out_specs=[IN_VMEM] * 4,
        out_shape=[jax.ShapeDtypeStruct((rows // 4, columns), BF16)] * 4,
        scratch_shapes=[pltpu.VMEM((rows, columns), F32)],
        compiler_params=params(rows),
        cost_estimate=cost(2 * rows * hidden * columns, 2 * hidden * columns + 10 * rows * hidden),
        name="teacher_down",
    )(*pres, down, payload)


def student_kernel(parts, inner, block, *refs):
    pre_refs, down_ref, teacher_refs = refs[:parts], refs[parts], refs[parts + 1 : parts + 5]
    hidden_ref, out_refs, total = refs[parts + 5], refs[parts + 6 : -1], refs[-1]
    for i in range(down_ref.shape[0] // block):
        here = slice(i * block, (i + 1) * block)
        hidden = activated(pre_refs, block, i)
        hidden_ref[:, here] = hidden
        term = plain(hidden, down_ref[here, :])
        if i == 0:
            total[...] = term
        else:
            total[...] += term
    first = out_refs[0].shape[0]
    for piece, near, part, place in teacher_places(total.shape[0], inner):
        block = (total[piece, :] - teacher_refs[part][place, :].astype(F32)).astype(BF16)
        if part < 2:
            out_refs[2 * near][...] = block[:first]
            out_refs[2 * near + 1][: block.shape[0] - first, :] = block[first:]
        else:
            out_refs[2 * near + 1][block.shape[0] - first :, :] = block


def student_parts(pres, down, teacher, inner, first):
    hidden, columns = down.shape
    rows, block = pres[0].shape[0], block_of(hidden, STUDENT_BLOCK)
    outs = pl.pallas_call(
        functools.partial(student_kernel, len(pres), inner, block),
        in_specs=[IN_VMEM] * (len(pres) + 5),
        out_specs=[IN_VMEM] * (1 + 2 * inner),
        out_shape=[jax.ShapeDtypeStruct((rows, hidden), BF16)]
        + [jax.ShapeDtypeStruct((height, columns), BF16) for height in (first, rows // inner - first)] * inner,
        scratch_shapes=[pltpu.VMEM((rows, columns), F32)],
        compiler_params=params(rows),
        cost_estimate=cost(2 * rows * hidden * columns, 2 * hidden * columns + 10 * rows * hidden),
        name="student_down",
    )(*pres, down, *teacher)
    return outs[0], outs[1::2], outs[2::2]


def hidden_grad_kernel(block, delta_ref, down_ref, out_ref):
    for i in range(out_ref.shape[1] // block):
        here = slice(i * block, (i + 1) * block)
        out_ref[:, here] = against(delta_ref[...], down_ref[here, :]).astype(BF16)


def hidden_grad_parts(delta, down):
    hidden, columns = down.shape
    rows = delta.shape[0]
    return pl.pallas_call(
        functools.partial(hidden_grad_kernel, block_of(hidden)),
        in_specs=[IN_VMEM] * 2,
        out_specs=IN_VMEM,
        out_shape=jax.ShapeDtypeStruct((rows, hidden), BF16),
        compiler_params=params(rows),
        cost_estimate=cost(2 * rows * hidden * columns, 2 * hidden * columns + 2 * rows * columns),
        name="hidden_grad",
    )(delta, down)


def grad_down_kernel(block, hidden_ref, delta_ref, out_hbm, out_ref, sems):
    copies = []
    for i in range(out_hbm.shape[0] // block):
        here = slice(i * block, (i + 1) * block)
        out_ref[here, :] = across(hidden_ref[:, here], delta_ref[...]).astype(BF16)
        copies.append(pltpu.make_async_copy(out_ref.at[here, :], out_hbm.at[here, :], sems.at[i]))
        copies[-1].start()
    for copy in copies:
        copy.wait()


def grad_down_of(hidden_rows, delta):
    rows, hidden = hidden_rows.shape
    columns, block = delta.shape[1], block_of(hidden, 256)
    return pl.pallas_call(
        functools.partial(grad_down_kernel, block),
        in_specs=[IN_VMEM] * 2,
        out_specs=IN_HBM,
        out_shape=jax.ShapeDtypeStruct((hidden, columns), BF16),
        scratch_shapes=[pltpu.VMEM((hidden, columns), BF16), pltpu.SemaphoreType.DMA((hidden // block,))],
        compiler_params=params(rows),
        cost_estimate=cost(2 * rows * hidden * columns, 2 * hidden * columns + 2 * rows * columns),
        name="grad_down",
    )(hidden_rows, delta)


def grad_pre_kernel(parts, block, *refs):
    pre_refs, back_refs, x_ref = refs[:parts], refs[parts : 2 * parts], refs[2 * parts]
    outs_hbm, out_refs, sems = refs[2 * parts + 1 : 2 * parts + 3], refs[-3:-1], refs[-1]
    columns = outs_hbm[0].shape[1]
    copies = []
    for i in range(outs_hbm[0].shape[0] // block):
        here = slice(i * block, (i + 1) * block)
        gate, up = added(pre_refs, block, i)
        back = back_refs[0][:, here].astype(F32)
        for ref in back_refs[1:]:
            back = back + ref[:, here].astype(F32)
        sig = jax.nn.sigmoid(gate)
        grads = (back * up * sig * (1.0 + gate * (1.0 - sig))).astype(BF16), (back * gate * sig).astype(BF16)
        for k in range(2):
            out_refs[k][here, :] = across(grads[k], x_ref[:, :columns]).astype(BF16)
            copies.append(pltpu.make_async_copy(out_refs[k].at[here, :], outs_hbm[k].at[here, :], sems.at[k, i]))
            copies[-1].start()
    for copy in copies:
        copy.wait()


def grad_pre_of(pres, backs, payload, columns):
    rows, hidden = backs[0].shape
    block = block_of(hidden, STUDENT_BLOCK)
    return pl.pallas_call(
        functools.partial(grad_pre_kernel, len(pres), block),
        in_specs=[IN_VMEM] * (2 * len(pres) + 1),
        out_specs=[IN_HBM] * 2,
        out_shape=[jax.ShapeDtypeStruct((hidden, columns), BF16)] * 2,
        scratch_shapes=[pltpu.VMEM((hidden, columns), BF16)] * 2 + [pltpu.SemaphoreType.DMA((2, hidden // block))],
        compiler_params=params(rows),
        cost_estimate=cost(4 * rows * hidden * columns, 4 * hidden * columns + 2 * rows * columns),
        name="grad_gate_up",
    )(*pres, *backs, payload)


def added_rows(one, other):
    return (one.astype(F32) + other.astype(F32)).astype(BF16)


def even_blocks(value, count):
    return value.reshape(count // 2, 2, -1, value.shape[1])[:, 0].reshape(-1, value.shape[1])


def odd_blocks(value, count):
    return value.reshape(count // 2, 2, -1, value.shape[1])[:, 1].reshape(-1, value.shape[1])


def shards(
    layer_in,
    route_ids,
    route_scores,
    expert_gate,
    expert_up,
    expert_down,
    student_gate,
    student_up,
    student_down,
):
    owners = lax.axis_size("wide")
    ring = Ring(owners)
    tok_rows, columns = layer_in.shape

    payload = make_payload(layer_in, route_ids, route_scores, owners)
    far = ring.gather_far_last(payload)
    far[-1] = passed(far[-1])
    far[-1], payload = lax.optimization_barrier((far[-1], payload))
    near = ring.gather_near(payload)
    column = jnp.concatenate(far, axis=0)
    rows = ring.joined(payload, near, column, ring.gather_near(column))

    expert_pre = pre_parts(rows, expert_gate[0], expert_up[0], BF16, TEACHER_BLOCK, "teacher_pre")
    expert_pres = [expert_pre] + from_pair(expert_pre)
    student_pre = pre_parts(rows, student_gate, student_up, F32, STUDENT_BLOCK, "student_pre")
    student_pres = [student_pre] + from_pair(student_pre)
    teacher = teacher_parts(expert_pres, expert_down[0], rows, ring.inner, owners)
    student_hidden, firsts, rests = student_parts(student_pres, student_down, teacher, ring.inner, tok_rows)

    loss_scale = 1.0 / math.sqrt(tok_rows * owners)
    column, teacher = lax.optimization_barrier((ring.reduce_near(rests), teacher))
    arrived = [ring.swap(teacher[2 * k + 1], 1 + k, 0) for k in range(2)]
    terms = ring.reduce_far([firsts[0]] + list(column.reshape(ring.outer - 1, tok_rows, columns)))
    terms += [ring.swap(firsts[k], k, 0) for k in range(1, ring.inner)]
    delta = (sum(a.astype(F32) for a in terms) * loss_scale).astype(BF16)
    delta, arrived = lax.optimization_barrier((delta, arrived))
    taught = [added_rows(teacher[2 * k], arrived[k]) for k in range(2)]

    far = ring.gather_far(delta)
    count = ring.inner // 2
    near = [
        ring.swap(jnp.concatenate([delta, odd_blocks(taught[2 - k], count)], axis=0), k, 0) for k in (1, 2)
    ]
    column = jnp.concatenate(far, axis=0)
    taught = [added_rows(even_blocks(taught[2 - k], count), near[k - 1][tok_rows:]) for k in (2, 1)]
    near = [block[:tok_rows] for block in near]
    bit = 4
    while bit < ring.inner:
        count //= 2
        taught = [added_rows(even_blocks(t, count), ring.swap(odd_blocks(t, count), bit, 0)) for t in taught]
        bit *= 2
    both = jnp.concatenate([delta, column], axis=0)
    rest = [ring.swap(column if k < 3 else both, k, 0) for k in range(1, ring.inner)]
    delta_all = jnp.concatenate([both, near[0], rest[0], near[1]] + rest[1:], axis=0)
    terms = ring.reduce_far(list(jnp.concatenate(taught, axis=0).reshape(ring.outer, tok_rows, columns)))
    delta_all, terms[0] = lax.optimization_barrier((delta_all, terms[0]))
    teacher_out = sum(a.astype(F32) for a in terms).astype(BF16)

    back = hidden_grad_parts(delta_all, student_down)
    backs = [back] + from_pair(back)
    grad_down = grad_down_of(student_hidden, delta_all)
    grad_gate, grad_up = grad_pre_of(student_pres, backs, rows, columns)
    return (teacher_out, grad_gate, grad_up, grad_down)


def solution(mesh):
    in_specs = (
        P("wide", "dp"),
        P("wide", None),
        P("wide", None),
        P("wide", None, "dp"),
        P("wide", None, "dp"),
        P("wide", None, "dp"),
        P("wide", "dp"),
        P("wide", "dp"),
        P("wide", "dp"),
    )
    out_specs = (P("wide", "dp"), P("wide", "dp"), P("wide", "dp"), P("wide", "dp"))
    return jax.shard_map(shards, mesh=mesh, in_specs=in_specs, out_specs=out_specs, check_vma=False)
```

```python
import functools
import math

import jax
import jax.numpy as jnp
from jax import lax
from jax.experimental import pallas as pl
from jax.experimental.pallas import tpu as pltpu
from jax.sharding import PartitionSpec as P

BF16 = jnp.bfloat16
F32 = jnp.float32
MIB = 1024 * 1024
IN_VMEM = pl.BlockSpec(memory_space=pltpu.VMEM)
IN_HBM = pl.BlockSpec(memory_space=pltpu.HBM)
LANES = 128
TEACHER_BLOCK = 768
STUDENT_BLOCK = 256


def against(left_mat, right_mat):
    return lax.dot_general(left_mat, right_mat, (((1,), (1,)), ((), ())), preferred_element_type=F32)


def across(left_mat, right_mat):
    return lax.dot_general(left_mat, right_mat, (((0,), (0,)), ((), ())), preferred_element_type=F32)


def plain(left_mat, right_mat):
    return lax.dot_general(left_mat, right_mat, (((1,), (0,)), ((), ())), preferred_element_type=F32)


def block_of(size, most=384):
    fits = [b for b in range(LANES, most + 1, LANES) if size % b == 0]
    return fits[-1] if fits else size


def params(rows):
    limit = min(18 * max(1, rows // 256), 56) * MIB
    return pltpu.CompilerParams(vmem_limit_bytes=limit)


def cost(flops, nbytes):
    return pl.CostEstimate(flops=int(flops), bytes_accessed=int(nbytes), transcendentals=0)


class Ring:
    def __init__(self, size):
        assert size & (size - 1) == 0 and size >= 4, size
        self.size, self.inner = size, 1 << (size.bit_length() - 1) // 2
        self.outer = size // self.inner

    def swap(self, value, near, far):
        flip = near + self.inner * far
        return lax.ppermute(value, "wide", [(i, i ^ flip) for i in range(self.size)])

    def gather_far(self, value):
        return [self.swap(value, 0, k) for k in range(1, self.outer)]

    def gather_far_last(self, value):
        return [self.swap(value, 0, k) for k in range(self.outer - 1, 0, -1)][::-1]

    def gather_near(self, value):
        return [self.swap(value, k, 0) for k in range(1, self.inner)]

    def joined(self, value, near, column, rest):
        blocks = [value, column]
        for first, others in zip(near, rest):
            blocks += [first, others]
        return jnp.concatenate(blocks, axis=0)

    def reduce_near(self, pieces, later):
        arrived = [self.swap(pieces[k], k, 0) for k in range(1, self.inner)]
        arrived[0], later = lax.optimization_barrier((arrived[0], later))
        return sum(a.astype(F32) for a in [pieces[0]] + arrived).astype(BF16), later

    def reduce_far(self, blocks):
        return [blocks[0]] + [self.swap(blocks[k], 0, k) for k in range(1, self.outer)]


def from_pair(value):
    size = lax.axis_size("dp")
    return [lax.ppermute(value, "dp", [(i, (i + s) % size) for i in range(size)]) for s in range(1, size)]


def payload_kernel(owners, layer_hbm, ids_hbm, scores_hbm, out_ref, ids_ref, scores_ref, sems):
    rows, columns = layer_hbm.shape
    copies = [
        pltpu.make_async_copy(ids_hbm, ids_ref, sems.at[0]),
        pltpu.make_async_copy(scores_hbm, scores_ref, sems.at[1]),
        pltpu.make_async_copy(layer_hbm, out_ref.at[:, pl.ds(0, columns)], sems.at[2]),
    ]
    for copy in copies:
        copy.start()
    copies[0].wait()
    copies[1].wait()
    scores = scores_ref[...]
    weights = scores / jnp.sum(scores, axis=0, keepdims=True)
    ids = ids_ref[...]
    shape = (out_ref.shape[1] - columns, rows)
    place = lax.broadcasted_iota(jnp.int32, shape, 0)
    expert = jnp.where(place >= owners, place - owners, place)
    table = jnp.zeros(shape, F32)
    for k in range(ids.shape[0]):
        table = table + jnp.where(ids[k : k + 1, :] == expert, weights[k : k + 1, :], 0.0)
    high = table.astype(BF16).astype(F32)
    table = jnp.where(place < owners, high, table - high)
    out_ref[:, columns:] = table.T.astype(BF16)
    copies[2].wait()


def make_payload(layer_in, route_ids, route_scores, owners):
    rows, columns = layer_in.shape
    extra = -(-2 * owners // LANES) * LANES
    return pl.pallas_call(
        functools.partial(payload_kernel, owners),
        in_specs=[IN_HBM] * 3,
        out_shape=jax.ShapeDtypeStruct((rows, columns + extra), BF16),
        scratch_shapes=[
            pltpu.VMEM(route_ids.shape[::-1], jnp.int32),
            pltpu.VMEM(route_scores.shape[::-1], F32),
            pltpu.SemaphoreType.DMA((3,)),
        ],
        compiler_params=pltpu.CompilerParams(vmem_limit_bytes=54 * MIB),
        name="payload",
    )(layer_in, route_ids.T, route_scores.T)


def pass_kernel(in_ref, out_ref):
    out_ref[...] = in_ref[...]


def passed(value):
    return pl.pallas_call(
        pass_kernel,
        out_shape=jax.ShapeDtypeStruct(value.shape, value.dtype),
        compiler_params=pltpu.CompilerParams(vmem_limit_bytes=2 * MIB),
        cost_estimate=cost(1e11, 1e5),
        name="passed",
    )(value)


def pre_kernel(block, x_ref, gate_ref, up_ref, out_ref):
    columns = gate_ref.shape[1]
    for i in range(gate_ref.shape[0] // block):
        here = slice(i * block, (i + 1) * block)
        for k, mat_ref in enumerate((gate_ref, up_ref)):
            there = slice((2 * i + k) * block, (2 * i + k + 1) * block)
            out_ref[:, there] = against(x_ref[:, :columns], mat_ref[here, :]).astype(out_ref.dtype)


def pre_parts(x, gate, up, dtype, most, name):
    hidden, columns = gate.shape
    rows, block = x.shape[0], block_of(hidden, most)
    return pl.pallas_call(
        functools.partial(pre_kernel, block),
        in_specs=[IN_VMEM] * 3,
        out_specs=IN_VMEM,
        out_shape=jax.ShapeDtypeStruct((rows, 2 * hidden), dtype),
        compiler_params=params(rows),
        cost_estimate=cost(4 * rows * hidden * columns, 4 * hidden * columns + 4 * rows * hidden),
        name=name,
    )(x, gate, up)


def added(refs, block, i):
    here = slice(2 * i * block, 2 * (i + 1) * block)
    total = refs[0][:, here].astype(F32)
    for ref in refs[1:]:
        total = total + ref[:, here].astype(F32)
    return total[:, :block], total[:, block:]


def activated(refs, block, i):
    gate, up = added(refs, block, i)
    return (gate * jax.nn.sigmoid(gate) * up).astype(BF16)


def teacher_places(rows, inner):
    length = rows // inner // 2
    for near in range(inner):
        for second in range(2):
            here = (2 * near + second) * length
            part = 2 + (near >> 1 & 1) if second else near & 1
            there = ((near >> 2) * 2 + (near & 1) if second else near >> 1) * length
            yield slice(here, here + length), near, part, slice(there, there + length)


def teacher_kernel(parts, inner, owners, block, *refs):
    pre_refs, down_ref, table_ref = refs[:parts], refs[parts], refs[parts + 1]
    out_refs, total = refs[parts + 2 : parts + 6], refs[-1]
    extra = table_ref.shape[1] - down_ref.shape[1]
    for i in range(down_ref.shape[0] // block):
        term = plain(activated(pre_refs, block, i), down_ref[i * block : (i + 1) * block, :])
        if i == 0:
            total[...] = term
        else:
            total[...] += term
    me = lax.axis_index("wide")
    table = table_ref[:, down_ref.shape[1] :].astype(F32)
    lane = lax.broadcasted_iota(jnp.int32, (table.shape[0], extra), 1)
    mine = (lane == me) | (lane == me + owners)
    weight = jnp.sum(jnp.where(mine, table, 0.0), axis=1, keepdims=True)
    for piece, _, part, place in teacher_places(total.shape[0], inner):
        out_refs[part][place, :] = (total[piece, :] * weight[piece, :]).astype(BF16)


def teacher_parts(pres, down, payload, inner, owners):
    hidden, columns = down.shape
    rows, block = payload.shape[0], block_of(hidden, TEACHER_BLOCK)
    return pl.pallas_call(
        functools.partial(teacher_kernel, len(pres), inner, owners, block),
        in_specs=[IN_VMEM] * (len(pres) + 2),
        out_specs=[IN_VMEM] * 4,
        out_shape=[jax.ShapeDtypeStruct((rows // 4, columns), BF16)] * 4,
        scratch_shapes=[pltpu.VMEM((rows, columns), F32)],
        compiler_params=params(rows),
        cost_estimate=cost(2 * rows * hidden * columns, 2 * hidden * columns + 10 * rows * hidden),
        name="teacher_down",
    )(*pres, down, payload)


def student_kernel(parts, inner, block, *refs):
    pre_refs, down_ref, teacher_refs = refs[:parts], refs[parts], refs[parts + 1 : parts + 5]
    hidden_ref, out_refs, total = refs[parts + 5], refs[parts + 6 : -1], refs[-1]
    for i in range(down_ref.shape[0] // block):
        here = slice(i * block, (i + 1) * block)
        hidden = activated(pre_refs, block, i)
        hidden_ref[:, here] = hidden
        term = plain(hidden, down_ref[here, :])
        if i == 0:
            total[...] = term
        else:
            total[...] += term
    first = out_refs[0].shape[0]
    for piece, near, part, place in teacher_places(total.shape[0], inner):
        block = (total[piece, :] - teacher_refs[part][place, :].astype(F32)).astype(BF16)
        if part < 2:
            out_refs[2 * near][...] = block[:first]
            out_refs[2 * near + 1][: block.shape[0] - first, :] = block[first:]
        else:
            out_refs[2 * near + 1][block.shape[0] - first :, :] = block


def student_parts(pres, down, teacher, inner, first):
    hidden, columns = down.shape
    rows, block = pres[0].shape[0], block_of(hidden, STUDENT_BLOCK)
    outs = pl.pallas_call(
        functools.partial(student_kernel, len(pres), inner, block),
        in_specs=[IN_VMEM] * (len(pres) + 5),
        out_specs=[IN_VMEM] * (1 + 2 * inner),
        out_shape=[jax.ShapeDtypeStruct((rows, hidden), BF16)]
        + [jax.ShapeDtypeStruct((height, columns), BF16) for height in (first, rows // inner - first)] * inner,
        scratch_shapes=[pltpu.VMEM((rows, columns), F32)],
        compiler_params=params(rows),
        cost_estimate=cost(2 * rows * hidden * columns, 2 * hidden * columns + 10 * rows * hidden),
        name="student_down",
    )(*pres, down, *teacher)
    return outs[0], outs[1::2], outs[2::2]


def hidden_grad_kernel(block, delta_ref, down_ref, out_ref):
    for i in range(out_ref.shape[1] // block):
        here = slice(i * block, (i + 1) * block)
        out_ref[:, here] = against(delta_ref[...], down_ref[here, :]).astype(BF16)


def hidden_grad_parts(delta, down):
    hidden, columns = down.shape
    rows = delta.shape[0]
    return pl.pallas_call(
        functools.partial(hidden_grad_kernel, block_of(hidden)),
        in_specs=[IN_VMEM] * 2,
        out_specs=IN_VMEM,
        out_shape=jax.ShapeDtypeStruct((rows, hidden), BF16),
        compiler_params=params(rows),
        cost_estimate=cost(2 * rows * hidden * columns, 2 * hidden * columns + 2 * rows * columns),
        name="hidden_grad",
    )(delta, down)


def grad_down_kernel(block, hidden_ref, delta_ref, out_hbm, out_ref, sems):
    copies = []
    for i in range(out_hbm.shape[0] // block):
        here = slice(i * block, (i + 1) * block)
        out_ref[here, :] = across(hidden_ref[:, here], delta_ref[...]).astype(BF16)
        copies.append(pltpu.make_async_copy(out_ref.at[here, :], out_hbm.at[here, :], sems.at[i]))
        copies[-1].start()
    for copy in copies:
        copy.wait()


def grad_down_of(hidden_rows, delta):
    rows, hidden = hidden_rows.shape
    columns, block = delta.shape[1], block_of(hidden, 256)
    return pl.pallas_call(
        functools.partial(grad_down_kernel, block),
        in_specs=[IN_VMEM] * 2,
        out_specs=IN_HBM,
        out_shape=jax.ShapeDtypeStruct((hidden, columns), BF16),
        scratch_shapes=[pltpu.VMEM((hidden, columns), BF16), pltpu.SemaphoreType.DMA((hidden // block,))],
        compiler_params=params(rows),
        cost_estimate=cost(2 * rows * hidden * columns, 2 * hidden * columns + 2 * rows * columns),
        name="grad_down",
    )(hidden_rows, delta)


def grad_pre_kernel(parts, block, *refs):
    pre_refs, back_refs, x_ref = refs[:parts], refs[parts : 2 * parts], refs[2 * parts]
    outs_hbm, out_refs, sems = refs[2 * parts + 1 : 2 * parts + 3], refs[-3:-1], refs[-1]
    columns = outs_hbm[0].shape[1]
    copies = []
    for i in range(outs_hbm[0].shape[0] // block):
        here = slice(i * block, (i + 1) * block)
        gate, up = added(pre_refs, block, i)
        back = back_refs[0][:, here].astype(F32)
        for ref in back_refs[1:]:
            back = back + ref[:, here].astype(F32)
        sig = jax.nn.sigmoid(gate)
        grads = (back * up * sig * (1.0 + gate * (1.0 - sig))).astype(BF16), (back * gate * sig).astype(BF16)
        for k in range(2):
            out_refs[k][here, :] = across(grads[k], x_ref[:, :columns]).astype(BF16)
            copies.append(pltpu.make_async_copy(out_refs[k].at[here, :], outs_hbm[k].at[here, :], sems.at[k, i]))
            copies[-1].start()
    for copy in copies:
        copy.wait()


def grad_pre_of(pres, backs, payload, columns):
    rows, hidden = backs[0].shape
    block = block_of(hidden, STUDENT_BLOCK)
    return pl.pallas_call(
        functools.partial(grad_pre_kernel, len(pres), block),
        in_specs=[IN_VMEM] * (2 * len(pres) + 1),
        out_specs=[IN_HBM] * 2,
        out_shape=[jax.ShapeDtypeStruct((hidden, columns), BF16)] * 2,
        scratch_shapes=[pltpu.VMEM((hidden, columns), BF16)] * 2 + [pltpu.SemaphoreType.DMA((2, hidden // block))],
        compiler_params=params(rows),
        cost_estimate=cost(4 * rows * hidden * columns, 4 * hidden * columns + 2 * rows * columns),
        name="grad_gate_up",
    )(*pres, *backs, payload)


def added_rows(one, other):
    return (one.astype(F32) + other.astype(F32)).astype(BF16)


def even_blocks(value, count):
    return value.reshape(count // 2, 2, -1, value.shape[1])[:, 0].reshape(-1, value.shape[1])


def odd_blocks(value, count):
    return value.reshape(count // 2, 2, -1, value.shape[1])[:, 1].reshape(-1, value.shape[1])


def shards(
    layer_in,
    route_ids,
    route_scores,
    expert_gate,
    expert_up,
    expert_down,
    student_gate,
    student_up,
    student_down,
):
    owners = lax.axis_size("wide")
    ring = Ring(owners)
    tok_rows, columns = layer_in.shape

    payload = make_payload(layer_in, route_ids, route_scores, owners)
    far = ring.gather_far_last(payload)
    far[-1] = passed(far[-1])
    far[-1], payload = lax.optimization_barrier((far[-1], payload))
    near = ring.gather_near(payload)
    column = jnp.concatenate(far, axis=0)
    rows = ring.joined(payload, near, column, ring.gather_near(column))

    expert_pre = pre_parts(rows, expert_gate[0], expert_up[0], BF16, TEACHER_BLOCK, "teacher_pre")
    expert_pres = [expert_pre] + from_pair(expert_pre)
    student_pre = pre_parts(rows, student_gate, student_up, F32, STUDENT_BLOCK, "student_pre")
    student_pres = [student_pre] + from_pair(student_pre)
    teacher = teacher_parts(expert_pres, expert_down[0], rows, ring.inner, owners)
    student_hidden, firsts, rests = student_parts(student_pres, student_down, teacher, ring.inner, tok_rows)

    loss_scale = 1.0 / math.sqrt(tok_rows * owners)
    column, firsts = ring.reduce_near(rests, firsts)
    column, teacher = lax.optimization_barrier((column, teacher))
    arrived = [ring.swap(teacher[2 * k + 1], 1 + k, 0) for k in range(2)]
    terms = ring.reduce_far([firsts[0]] + list(column.reshape(ring.outer - 1, tok_rows, columns)))
    terms += [ring.swap(firsts[k], k, 0) for k in range(1, ring.inner)]
    delta = (sum(a.astype(F32) for a in terms) * loss_scale).astype(BF16)
    delta, arrived = lax.optimization_barrier((delta, arrived))
    taught = [added_rows(teacher[2 * k], arrived[k]) for k in range(2)]

    far = ring.gather_far(delta)
    count = ring.inner // 2
    near = [
        ring.swap(jnp.concatenate([delta, odd_blocks(taught[2 - k], count)], axis=0), k, 0) for k in (1, 2)
    ]
    column = jnp.concatenate(far, axis=0)
    taught = [added_rows(even_blocks(taught[2 - k], count), near[k - 1][tok_rows:]) for k in (2, 1)]
    near = [block[:tok_rows] for block in near]
    bit = 4
    while bit < ring.inner:
        count //= 2
        taught = [added_rows(even_blocks(t, count), ring.swap(odd_blocks(t, count), bit, 0)) for t in taught]
        bit *= 2
    both = jnp.concatenate([delta, column], axis=0)
    rest = [ring.swap(column if k < 3 else both, k, 0) for k in range(1, ring.inner)]
    delta_all = jnp.concatenate([both, near[0], rest[0], near[1]] + rest[1:], axis=0)
    terms = ring.reduce_far(list(jnp.concatenate(taught, axis=0).reshape(ring.outer, tok_rows, columns)))
    delta_all, terms[0] = lax.optimization_barrier((delta_all, terms[0]))
    teacher_out = sum(a.astype(F32) for a in terms).astype(BF16)

    back = hidden_grad_parts(delta_all, student_down)
    backs = [back] + from_pair(back)
    grad_down = grad_down_of(student_hidden, delta_all)
    grad_gate, grad_up = grad_pre_of(student_pres, backs, rows, columns)
    return (teacher_out, grad_gate, grad_up, grad_down)


def solution(mesh):
    in_specs = (
        P("wide", "dp"),
        P("wide", None),
        P("wide", None),
        P("wide", None, "dp"),
        P("wide", None, "dp"),
        P("wide", None, "dp"),
        P("wide", "dp"),
        P("wide", "dp"),
        P("wide", "dp"),
    )
    out_specs = (P("wide", "dp"), P("wide", "dp"), P("wide", "dp"), P("wide", "dp"))
    return jax.shard_map(shards, mesh=mesh, in_specs=in_specs, out_specs=out_specs, check_vma=False)
```
